256 devices in a mesh: ctx: 32 (over y, z_hi, core), exp: 8 (over z_lo, x).
Axes of the slice: x: 4, y: 4, z: 8 (z_hi: 4, z_lo: 2; z = z_hi * 2 + z_lo), core: 2. Of those that a mesh axis runs over, the one named last changes fastest.
Arguments:
- residual: bfloat16 [4096, 2048], P(('ctx', 'exp')), may hold values from -11 to 11
- query_states: bfloat16 [4096, 2048], P('ctx', 'exp'), may hold values from -14 to 14
- key_states: bfloat16 [4096, 2048], P('ctx', 'exp'), may hold values from -14 to 14
- value_states: bfloat16 [4096, 2048], P('ctx', 'exp'), may hold values from -6 to 6
- out_weight: bfloat16 [2048, 2048], P('exp'), may hold values from -0.125 to 0.125
- norm_gain: float32 [2048], replicated, may hold values from 0.25 to 1.75
- expert_ids: int32 [4096, 2], P(('ctx', 'exp')), may hold values from 0 to 15, all different within a row
- gate_weights: float32 [4096, 2], P(('ctx', 'exp')), may hold values from 0.2 to 1
- gate_matrix: bfloat16 [16, 2048, 6400], P('exp', None, 'ctx'), may hold values from -0.125 to 0.125
- up_matrix: bfloat16 [16, 2048, 6400], P('exp', None, 'ctx'), may hold values from -0.125 to 0.125
- down_matrix: bfloat16 [16, 6400, 2048], P('exp', 'ctx'), may hold values from -0.078125 to 0.078125
- grad_out: bfloat16 [4096, 2048], P(('ctx', 'exp')), may hold values from -6 to 6
Outputs:
- layer_out: bfloat16 [4096, 2048], P(('ctx', 'exp'))
- grad_residual: bfloat16 [4096, 2048], P(('ctx', 'exp'))
- grad_query: bfloat16 [4096, 2048], P('ctx', 'exp')
- grad_keys: bfloat16 [4096, 2048], P('ctx', 'exp')
- grad_values: bfloat16 [4096, 2048], P('ctx', 'exp')
The draws below stay inside these ranges and needn't reach their ends.
Inputs may be any that keep to these rules, and one draw needn't show every extreme that they name: `expert_ids`: each row names 2 different experts.
All inputs are finite; a program needn't handle non-finite values.
Results may differ from the reference program's by a relative error of at most 0.04.
Values may be sent and summed in bfloat16 or wider, within the bound.
A program may use at most 128 MiB of HBM per device.

```python
import math
import jax
import jax.numpy as jnp
from jax import lax

D = 2048
HEADS = 16
HD = 128
FF = 6400
E = 16
TOP = 2
LEN = 4096
ROWS = 16
CAP = 2
N_CTX = 32
N_EXP = 8


def draw_query_states(key, part):
    key = jax.random.fold_in(key, 5)
    result = 1.5 * jnp.clip(jax.random.normal(key, (LEN, HEADS * HD), jnp.float32), -3.0, 3.0)
    return result.astype(jnp.bfloat16)


def draw_key_states(key, part):
    key = jax.random.fold_in(key, 7)
    result = 1.5 * jnp.clip(jax.random.normal(key, (LEN, HEADS * HD), jnp.float32), -3.0, 3.0)
    return result.astype(jnp.bfloat16)


def draw_residual(key, part):
    key = jax.random.fold_in(key, 9)
    row_key, column_key, main_key = jax.random.split(key, 3)
    row_scale = jnp.exp(jax.random.uniform(row_key, (LEN, 1), jnp.float32, math.log(0.3), math.log(3.0)))
    column_scale = jnp.exp(jax.random.uniform(column_key, (1, D), jnp.float32, math.log(0.3), math.log(3.0)))
    main_part = jnp.clip(jax.random.normal(main_key, (LEN, D), jnp.float32), -4.0, 4.0)
    result = 0.3 * main_part * row_scale * column_scale
    return result.astype(jnp.bfloat16)


def level_of(rng, dims, pieces, least, largest):
    gain, own = 1.0, jax.random.fold_in(rng, 6)
    for dim, parts in pieces:
        heights = jnp.exp(jax.random.uniform(jax.random.fold_in(own, dim), (parts,), jnp.float32, least / len(pieces), largest / len(pieces)))
        gain = gain * jnp.repeat(heights, dims[dim] // parts).reshape([-1 if axis == dim else 1 for axis in range(len(dims))])
    return gain


def different_ones(key, rows, number_of, top, lift):
    ranking = jax.random.permutation(jax.random.fold_in(key, 1), number_of)
    boost = ranking
    for power in range(3):
        boost = boost * boost // number_of
    boost = boost * lift // number_of
    tickets = jax.random.randint(jax.random.fold_in(key, 2), (rows, number_of), 0, 4096) + boost
    sure = jax.random.permutation(jax.random.fold_in(key, 3), rows)[jnp.arange(number_of) % rows]
    tickets = jnp.where(jnp.arange(rows)[:, None] == sure[None, :], 1 << 14, tickets)
    merit = tickets * number_of + jnp.arange(number_of)
    return lax.top_k(merit.astype(jnp.int32), top)[1].astype(jnp.int32)


def bell_draw(own_key, shape, deviation, limit, pieces=(), kind=jnp.bfloat16):
    values = deviation * jax.random.normal(own_key, shape, jnp.float32)
    if pieces:
        values = values * level_of(own_key, shape, pieces, -0.22, 0.18)
    return jnp.clip(values, -limit, limit).astype(kind)


def setup_inputs(seed: int = 0) -> dict:
    seeds = jax.random.split(jax.random.key(seed), 13)
    return {
        "residual": draw_residual(jax.random.fold_in(seeds[12], 71), 0),
        "query_states": draw_query_states(jax.random.fold_in(seeds[12], 71), 0),
        "key_states": draw_key_states(jax.random.fold_in(seeds[12], 71), 0),
        "value_states": bell_draw(seeds[3], (LEN, HEADS * HD), 1.5, 6.0, ((0, 32), (1, 8))),
        "out_weight": bell_draw(seeds[4], (HEADS * HD, D), (HEADS * HD) ** -0.5, 0.125, ((0, 8),)),
        "norm_gain": jnp.clip(1.0 + 0.15 * jax.random.normal(seeds[5], (D,), jnp.float32), 0.25, 1.75),
        "expert_ids": different_ones(seeds[6], LEN, E, TOP, 2048),
        "gate_weights": jnp.clip(0.2 + 0.8 * jax.random.uniform(seeds[7], (LEN, TOP), jnp.float32) ** level_of(seeds[7], (LEN, TOP), ((0, 256),), -0.2, 0.2), 0.2, 1.0),
        "gate_matrix": bell_draw(seeds[8], (E, D, FF), D ** -0.5, 0.125, ((0, 8), (2, 32))),
        "up_matrix": bell_draw(seeds[9], (E, D, FF), D ** -0.5, 0.125, ((0, 8), (2, 32))),
        "down_matrix": bell_draw(seeds[10], (E, FF, D), FF ** -0.5, 0.078125, ((0, 8), (1, 32))),
        "grad_out": bell_draw(seeds[11], (LEN, D), 1.0, 6.0, ((0, 256),)),
    }


EPSILON = 1e-05
MASKED = -1e+30

def rounded(array):
    return lax.optimization_barrier(array.astype(jnp.bfloat16))

def matmul(left, right):
    return jnp.dot(left.astype(jnp.float32), right.astype(jnp.float32), precision=lax.Precision.HIGHEST, preferred_element_type=jnp.float32)

def head_scores(query_head, key_head):
    scale_factor = 1.0 / math.sqrt(HD)
    positions = lax.iota(jnp.int32, LEN)
    allowed = positions[None, :] <= positions[:, None]
    scores = matmul(query_head, key_head.T) * scale_factor
    return jnp.where(allowed, scores, MASKED)

def head_forward(query_head, key_head, value_head):
    scores = head_scores(query_head, key_head)
    row_max = lax.optimization_barrier(jnp.max(scores, axis=1, keepdims=True))
    log_total = row_max + jnp.log(lax.optimization_barrier(jnp.sum(jnp.exp(scores - row_max), axis=1, keepdims=True)))
    softmax = jnp.exp(scores - log_total)
    attended = rounded(matmul(rounded(softmax), value_head))
    return (attended, log_total)

def head_backward(query_head, key_head, value_head, attended, log_total, grad_head):
    scale_factor = 1.0 / math.sqrt(HD)
    scores = head_scores(query_head, key_head)
    softmax = jnp.exp(scores - log_total)
    row_delta = lax.optimization_barrier(jnp.sum(grad_head.astype(jnp.float32) * attended.astype(jnp.float32), axis=1, keepdims=True))
    grad_prob = matmul(grad_head, value_head.T)
    grad_score = rounded(softmax * (grad_prob - row_delta))
    grad_query = (matmul(grad_score, key_head) * scale_factor).astype(jnp.bfloat16)
    grad_keys = (matmul(grad_score.T, query_head) * scale_factor).astype(jnp.bfloat16)
    grad_values = matmul(rounded(softmax).T, grad_head).astype(jnp.bfloat16)
    return (grad_query, grad_keys, grad_values)

def expert_pass(packed):
    inputs_rows, grads_rows, gate_mat, up_mat, down_mat = packed
    gate_part = matmul(inputs_rows, gate_mat)
    up_part = matmul(inputs_rows, up_mat)
    sigmoid_part = jax.nn.sigmoid(gate_part)
    active = rounded(gate_part * sigmoid_part * up_part)
    grad_active = matmul(grads_rows, down_mat.T)
    grad_gate = rounded(grad_active * up_part * sigmoid_part * (1.0 + gate_part * (1.0 - sigmoid_part)))
    grad_up = rounded(grad_active * gate_part * sigmoid_part)
    group_size = FF // N_CTX
    slot_count = inputs_rows.shape[0]

    def add_group(totals, group_index):
        out_total, grad_total = totals
        offset = (group_index * group_size).astype(jnp.int32)
        active_part = lax.dynamic_slice_in_dim(active, offset, group_size, 1)
        gate_piece = lax.dynamic_slice_in_dim(grad_gate, offset, group_size, 1)
        up_piece = lax.dynamic_slice_in_dim(grad_up, offset, group_size, 1)
        down_rows = lax.dynamic_slice_in_dim(down_mat, offset, group_size, 0)
        gate_cols = lax.dynamic_slice_in_dim(gate_mat, offset, group_size, 1)
        up_cols = lax.dynamic_slice_in_dim(up_mat, offset, group_size, 1)
        out_piece = rounded(matmul(active_part, down_rows))
        grad_piece = rounded(matmul(gate_piece, gate_cols.T) + matmul(up_piece, up_cols.T))
        return ((out_total + out_piece.astype(jnp.float32), grad_total + grad_piece.astype(jnp.float32)), None)
    zeros_start = jnp.zeros((slot_count, D), jnp.float32)
    (out_total, grad_total), _ = lax.scan(add_group, (zeros_start, zeros_start), jnp.arange(N_CTX, dtype=jnp.int32))
    return (out_total.astype(jnp.bfloat16), grad_total.astype(jnp.bfloat16))

def reference(residual, query_states, key_states, value_states, out_weight, norm_gain, expert_ids, gate_weights, gate_matrix, up_matrix, down_matrix, grad_out):
    query_heads = query_states.reshape(LEN, HEADS, HD).transpose(1, 0, 2)
    key_heads = key_states.reshape(LEN, HEADS, HD).transpose(1, 0, 2)
    value_heads = value_states.reshape(LEN, HEADS, HD).transpose(1, 0, 2)
    attended, log_total = lax.map(lambda packed: head_forward(*packed), (query_heads, key_heads, value_heads))
    attended_rows = attended.transpose(1, 0, 2).reshape(LEN, HEADS * HD)
    projected = matmul(attended_rows, out_weight)
    hidden_state = rounded(residual.astype(jnp.float32) + projected)
    hidden_wide = hidden_state.astype(jnp.float32)
    inverse_norm = lax.rsqrt(lax.optimization_barrier(jnp.mean(hidden_wide * hidden_wide, axis=1, keepdims=True)) + EPSILON)
    normed = rounded(hidden_wide * inverse_norm * norm_gain)
    devices = N_CTX * N_EXP
    block_experts = expert_ids.reshape(devices, ROWS * TOP)
    chosen = (block_experts[:, :, None] == lax.iota(jnp.int32, E)[None, None, :]).astype(jnp.int32)
    earlier = jnp.cumsum(chosen, axis=1, dtype=jnp.int32) - chosen
    rank_index = lax.optimization_barrier(jnp.sum(earlier * chosen, axis=2, dtype=jnp.int32))
    kept = rank_index < CAP
    column = jnp.where(kept, lax.iota(jnp.int32, devices)[:, None] * CAP + rank_index, devices * CAP).astype(jnp.int32)
    flat_index = lax.iota(jnp.int32, LEN * TOP).reshape(devices, ROWS * TOP)
    slot_flat = jnp.full((E, devices * CAP), LEN * TOP, jnp.int32).at[block_experts, column].set(flat_index, mode='drop')
    weighted = rounded(gate_weights[:, :, None] * grad_out.astype(jnp.float32)[:, None, :]).reshape(LEN * TOP, D)
    inputs_all = jnp.take(normed, slot_flat // TOP, axis=0, mode='fill', fill_value=0)
    grads_all = jnp.take(weighted, slot_flat, axis=0, mode='fill', fill_value=0)
    slot_outputs, slot_grads = lax.map(expert_pass, (inputs_all, grads_all, gate_matrix, up_matrix, down_matrix))
    flat_slots = slot_flat.reshape(-1)
    out_flat = jnp.zeros((LEN * TOP, D), jnp.bfloat16).at[flat_slots].set(slot_outputs.reshape(-1, D), mode='drop').reshape(LEN, TOP, D)
    grad_flat = jnp.zeros((LEN * TOP, D), jnp.bfloat16).at[flat_slots].set(slot_grads.reshape(-1, D), mode='drop').reshape(LEN, TOP, D)
    mixture = lax.optimization_barrier(jnp.sum(gate_weights[:, :, None] * out_flat.astype(jnp.float32), axis=1))
    layer_out = (hidden_wide + mixture).astype(jnp.bfloat16)
    grad_normed = lax.optimization_barrier(jnp.sum(grad_flat.astype(jnp.float32), axis=1))
    scaled_grad = norm_gain * grad_normed
    inverse_cube = inverse_norm * inverse_norm * inverse_norm
    grad_hidden = grad_out.astype(jnp.float32) + (inverse_norm * scaled_grad - hidden_wide * inverse_cube * lax.optimization_barrier(jnp.mean(hidden_wide * scaled_grad, axis=1, keepdims=True)))
    grad_residual = rounded(grad_hidden)
    grad_attended = rounded(matmul(grad_residual, out_weight.T))
    grad_heads = grad_attended.reshape(LEN, HEADS, HD).transpose(1, 0, 2)
    grad_query, grad_keys, grad_values = lax.map(lambda packed: head_backward(*packed), (query_heads, key_heads, value_heads, attended, log_total, grad_heads))
    grad_query = grad_query.transpose(1, 0, 2).reshape(LEN, HEADS * HD)
    grad_keys = grad_keys.transpose(1, 0, 2).reshape(LEN, HEADS * HD)
    grad_values = grad_values.transpose(1, 0, 2).reshape(LEN, HEADS * HD)
    return (layer_out, grad_residual.astype(jnp.bfloat16), grad_query, grad_keys, grad_values)
```

```python
import functools
import math

import jax
import jax.numpy as jnp
from jax import lax
from jax.experimental import pallas as pl
from jax.experimental.pallas import tpu as pltpu
from jax.sharding import PartitionSpec as P

MESH = pl.DeviceIdType.MESH
F32 = jnp.float32
BF16 = jnp.bfloat16
HD = 128
D = 2048
ROWS = 16
CHIPS = 16
N_EXP = 8
CHIP_ROWS = 256
HIDDEN = 200
CHUNK = 1024
EPSILON = 1e-05
MASKED = -1e30
SCALE = 1.0 / math.sqrt(HD)
VMEM_LIMIT = 58 * 1024 * 1024
NT = (((1,), (1,)), ((), ()))
TN = (((0,), (0,)), ((), ()))


def rel(dy, dz):
    return dy * 4 + dz


class Net:
    def __init__(self, send, recv):
        self.send, self.recv, self.count, self.started = send, recv, 0, []
        ctx = lax.axis_index("ctx")
        self.exp = lax.axis_index("exp")
        self.core = lax.rem(ctx, 2)
        chip = ctx // 2
        self.y, self.z = chip // 4, lax.rem(chip, 4)
        at = lambda y, z, c: {"ctx": (lax.rem(y, 4) * 4 + lax.rem(z, 4)) * 2 + c}
        self.yp = at(self.y + 1, self.z, self.core)
        self.ym = at(self.y + 3, self.z, self.core)
        self.zp = at(self.y, self.z + 1, self.core)
        self.zm = at(self.y, self.z + 3, self.core)
        self.sibling = at(self.y, self.z, 1 - self.core)
        self.peers = [lax.rem(self.exp + d, N_EXP) for d in range(1, N_EXP)]

    def copy(self, src, dst, device):
        i = self.count
        self.count += 1
        made = pltpu.make_async_remote_copy(
            src_ref=src,
            dst_ref=dst,
            send_sem=self.send.at[i],
            recv_sem=self.recv.at[i],
            device_id=device,
            device_id_type=MESH,
        )
        made.start()
        self.started.append(made)
        return made

    def finish(self):
        for made in self.started:
            made.wait_send()

    def barrier(self, devices):
        sem = pltpu.get_barrier_semaphore()
        for device in devices:
            pl.semaphore_signal(sem, inc=1, device_id=device, device_id_type=MESH)
        pl.semaphore_wait(sem, len(devices))

    def ring_devices(self):
        return [self.yp, self.ym, self.zp, self.zm]

    def peer_devices(self):
        return [{"exp": peer} for peer in self.peers]

    def push(self, src_of, dst):
        return [self.copy(src_of(peer), dst, {"exp": peer}) for peer in self.peers]


def gather_steps(net, full, half, seen):
    state = {}

    def send_z():
        state["z3"] = net.copy(full(rel(0, 0)), full(rel(0, 3)), net.zp)
        state["z1"] = net.copy(full(rel(0, 0)), full(rel(0, 1)), net.zm)

    def send_y(dz):
        state["y3", dz] = net.copy(full(rel(0, dz)), full(rel(3, dz)), net.yp)
        state["y1", dz] = net.copy(full(rel(0, dz)), full(rel(1, dz)), net.ym)

    def near_z3():
        state["z3"].wait_recv()
        state["h0"] = net.copy(half(rel(0, 3), 0), half(rel(0, 2), 0), net.zp)
        send_y(3)
        seen(rel(0, 3))

    def near_z1():
        state["z1"].wait_recv()
        state["h1"] = net.copy(half(rel(0, 1), 1), half(rel(0, 2), 1), net.zm)
        send_y(1)
        seen(rel(0, 1))

    def far_z():
        state["h0"].wait_recv()
        state["h1"].wait_recv()
        send_y(2)
        seen(rel(0, 2))

    def near_y(dz):
        state["y3", dz].wait_recv()
        state["g0", dz] = net.copy(half(rel(3, dz), 0), half(rel(2, dz), 0), net.yp)
        state["y1", dz].wait_recv()
        state["g1", dz] = net.copy(half(rel(1, dz), 1), half(rel(2, dz), 1), net.ym)
        seen(rel(3, dz))
        seen(rel(1, dz))

    def far_y(dz):
        state["g0", dz].wait_recv()
        state["g1", dz].wait_recv()
        seen(rel(2, dz))

    first = [send_z, lambda: send_y(0)]
    relays = [near_z3, near_z1, lambda: near_y(0), far_z]
    relays += [lambda dz=dz: near_y(dz) for dz in (3, 1, 2)]
    last = [lambda dz=dz: far_y(dz) for dz in (0, 3, 1, 2)]
    return first, relays, last


def reduce_steps(net, full, half, near, far, load, store):
    ra, rb, za, zb = far
    rc, rd, zc, zd = near
    state = {}

    def send_far(dz):
        state["a", dz] = net.copy(half(rel(2, dz), 0), ra.at[dz], net.yp)
        state["b", dz] = net.copy(half(rel(2, dz), 1), rb.at[dz], net.ym)

    def add(target, *sources):
        total = load(target)
        for source in sources:
            total = total + load(source)
        store(target, total)

    def send_near(dz):
        state["a", dz].wait_recv()
        add(half(rel(1, dz), 0), ra.at[dz])
        state["c", dz] = net.copy(full(rel(1, dz)), rc.at[dz], net.yp)
        state["b", dz].wait_recv()
        add(half(rel(3, dz), 1), rb.at[dz])
        state["d", dz] = net.copy(full(rel(3, dz)), rd.at[dz], net.ym)

    def collect(dz):
        state["c", dz].wait_recv()
        state["d", dz].wait_recv()
        add(full(rel(0, dz)), rc.at[dz], rd.at[dz])
        if dz == 2:
            state["za"] = net.copy(half(rel(0, 2), 0), za, net.zp)
            state["zb"] = net.copy(half(rel(0, 2), 1), zb, net.zm)
        if dz == 1:
            state["za"].wait_recv()
            add(half(rel(0, 1), 0), za)
            state["zc"] = net.copy(full(rel(0, 1)), zc, net.zp)
        if dz == 3:
            state["zb"].wait_recv()
            add(half(rel(0, 3), 1), zb)
            state["zd"] = net.copy(full(rel(0, 3)), zd, net.zm)

    def last():
        state["zc"].wait_recv()
        state["zd"].wait_recv()
        add(full(rel(0, 0)), zc, zd)

    order = (2, 1, 3, 0)
    first = [lambda dz=dz: send_far(dz) for dz in order]
    rest = [lambda dz=dz: send_near(dz) for dz in order]
    rest += [lambda dz=dz: collect(dz) for dz in order]
    rest += [last]
    return first, rest


def merge(left, right):
    steps = [((i + 0.5) / len(left), 0, i) for i in range(len(left))]
    steps += [((i + 0.5) / len(right), 1, i) for i in range(len(right))]
    for _, side, i in sorted(steps):
        (left, right)[side][i]()


def load_wide(ref):
    return ref[...].astype(F32)


def store_narrow(ref, value):
    ref[...] = value.astype(BF16)


def column(ref, k):
    diagonal = lax.broadcasted_iota(jnp.int32, (ROWS, ROWS), 0) == lax.broadcasted_iota(
        jnp.int32, (ROWS, ROWS), 1
    )
    row = jnp.broadcast_to(ref[k : k + 1, :], (ROWS, ROWS))
    return jnp.sum(jnp.where(diagonal, row, jnp.zeros_like(row)), axis=1, keepdims=True)


def places(ids_ref):
    lanes = lax.broadcasted_iota(jnp.int32, (ROWS, 128), 1)
    ids = [column(ids_ref, k) for k in range(2)]
    chosen = [(lanes == one).astype(F32) for one in ids]
    lower = (
        lax.broadcasted_iota(jnp.int32, (ROWS, ROWS), 1)
        < lax.broadcasted_iota(jnp.int32, (ROWS, ROWS), 0)
    ).astype(BF16)
    earlier = jnp.dot(lower, (chosen[0] + chosen[1]).astype(BF16), preferred_element_type=F32)
    found = []
    for one, hot in zip(ids, chosen):
        rank = jnp.sum(earlier * hot, axis=1, keepdims=True).astype(jnp.int32)
        place = (one >> 1) * 16 + (one & 1) * 2 + rank
        found.append(jnp.where(rank < 2, place, -1000))
    return found


def one_hot(place, quarter):
    lanes = lax.broadcasted_iota(jnp.int32, (ROWS, 128), 1)
    return (lanes == place + 4 * quarter).astype(BF16)


def packing(quarter, transposed):
    shape, slot_dim = ((128, 32), 1) if transposed else ((32, 128), 0)
    slot = lax.broadcasted_iota(jnp.int32, shape, slot_dim)
    packed = lax.broadcasted_iota(jnp.int32, shape, 1 - slot_dim)
    want = ((slot & 15) >> 1) * 16 + quarter * 4 + (slot >> 4) * 2 + (slot & 1)
    return (packed == want).astype(BF16)


def forward_kernel(
    q_ref,
    k_ref,
    v_ref,
    ow_ref,
    residual_ref,
    gain_ref,
    ids_ref,
    gw_ref,
    go_ref,
    wg_ref,
    wu_ref,
    wd_ref,
    q_out,
    kv_out,
    p_out,
    att_out,
    hidden_out,
    arrived_out,
    wg_out,
    wu_out,
    wd_out,
    scores,
    att_pair,
    partial,
    pieces,
    packed,
    send,
    recv,
):
    net = Net(send, recv)
    core = net.core
    own_rows = pl.ds(pl.multiple_of(core * 128, 128), 128)
    own_values = pl.ds(pl.multiple_of(256 + core * 128, 128), 128)
    other_rows = pl.ds(pl.multiple_of((1 - core) * 128, 128), 128)
    net.barrier(net.ring_devices() + [net.sibling] + net.peer_devices())

    exchange = [
        net.copy(k_ref.at[:, other_rows], kv_out.at[0, own_rows, :], net.sibling),
        net.copy(v_ref.at[:, other_rows], kv_out.at[0, own_values, :], net.sibling),
        net.copy(q_ref.at[:, other_rows], q_out.at[own_rows, :], net.sibling),
    ]

    def mine(ref):
        return jnp.where(core == 0, ref[:, :128], ref[:, 128:])

    kv_out[0, own_rows, :] = mine(k_ref)
    kv_out[0, own_values, :] = mine(v_ref)
    q_out[own_rows, :] = mine(q_ref)

    chip = net.y * 4 + net.z

    def score_block(r):
        dy, dz = r // 4, r % 4
        other = lax.rem(net.y + dy, 4) * 4 + lax.rem(net.z + dz, 4)
        s = (
            lax.dot_general(q_out[...], kv_out[r, :256, :], NT, preferred_element_type=F32)
            * SCALE
        )
        row = lax.broadcasted_iota(jnp.int32, (CHIP_ROWS, CHIP_ROWS), 0) + chip * CHIP_ROWS
        column = lax.broadcasted_iota(jnp.int32, (CHIP_ROWS, CHIP_ROWS), 1) + other * CHIP_ROWS
        scores[r] = jnp.where(column <= row, s, MASKED)

    first, relays, last = gather_steps(
        net,
        lambda r: kv_out.at[r],
        lambda r, h: kv_out.at[r, pl.ds(h * 256, 256), :],
        score_block,
    )
    for made in exchange[:2]:
        made.wait_recv()
    for step in first:
        step()
    weights = [
        net.copy(wg_ref, wg_out, net.sibling),
        net.copy(wu_ref, wu_out, net.sibling),
        net.copy(wd_ref, wd_out, net.sibling),
    ]
    exchange[2].wait_recv()
    score_block(0)
    for step in relays + last:
        step()

    def top(r, m):
        s = scores[r]
        return jnp.maximum(m, jnp.maximum(s[:, :128], s[:, 128:]))

    m = lax.fori_loop(0, CHIPS, top, jnp.full((CHIP_ROWS, 128), MASKED, F32))
    m = jnp.max(m, axis=1, keepdims=True)

    def raise_all(r, total):
        e = jnp.exp(scores[r] - m)
        scores[r] = e
        return total + (e[:, :128] + e[:, 128:])

    total = lax.fori_loop(0, CHIPS, raise_all, jnp.zeros((CHIP_ROWS, 128), F32))
    inverse = 1.0 / jnp.sum(total, axis=1, keepdims=True)

    def attend(r, acc):
        low = (scores[r] * inverse).astype(BF16)
        p_out[r] = low
        return acc + jnp.dot(low, kv_out[r, 256:, :], preferred_element_type=F32)

    attended = lax.fori_loop(0, CHIPS, attend, jnp.zeros((CHIP_ROWS, HD), F32))
    att_out[...] = attended.astype(BF16)
    swap = net.copy(att_out.at[other_rows, :], att_pair.at[core], net.sibling)
    att_pair[core] = att_out[own_rows, :]
    swap.wait_recv()

    for n in range(4):
        columns = pl.ds(n * 512, 512)
        partial[:, columns] = (
            jnp.dot(att_pair[0], ow_ref[:128, columns], preferred_element_type=F32)
            + jnp.dot(att_pair[1], ow_ref[128:, columns], preferred_element_type=F32)
        ).astype(BF16)

    def piece(ref, peer):
        return ref.at[pl.ds(pl.multiple_of(peer * ROWS, ROWS), ROWS), :]

    me = net.exp
    moved = net.push(lambda peer: piece(partial, peer), piece(pieces, me))
    piece(pieces, me)[...] = piece(partial, me)[...]
    found = places(ids_ref)
    go = go_ref[...].astype(F32)
    weighted = [(column(gw_ref, k) * go).astype(BF16) for k in range(2)]
    for made in moved:
        made.wait_recv()
    projected = pieces[0:ROWS, :].astype(F32)
    for j in range(1, N_EXP):
        projected = projected + pieces[j * ROWS : (j + 1) * ROWS, :].astype(F32)
    hidden = (residual_ref[...].astype(F32) + projected).astype(BF16)
    hidden_out[...] = hidden
    wide = hidden.astype(F32)
    inverse_norm = lax.rsqrt(jnp.mean(wide * wide, axis=1, keepdims=True) + EPSILON)
    normed = (wide * inverse_norm * gain_ref[...]).astype(BF16)
    spread = jnp.zeros((128, CHUNK), F32)
    for quarter in range(4):
        for k in range(2):
            source = normed if quarter < 2 else weighted[k]
            low = (quarter % 2) * CHUNK
            spread = spread + lax.dot_general(
                one_hot(found[k], quarter),
                source[:, low : low + CHUNK],
                TN,
                preferred_element_type=F32,
            )
    packed[...] = spread.astype(BF16)
    moved = net.push(lambda peer: piece(packed, peer), piece(arrived_out, me))
    piece(arrived_out, me)[...] = piece(packed, me)[...]
    for made in moved + weights:
        made.wait_recv()
    net.finish()


def expert_kernel(
    arrived_ref,
    hidden_ref,
    gain_ref,
    ids_ref,
    gw_ref,
    go_ref,
    wg_ref,
    wu_ref,
    wd_ref,
    wg_other,
    wu_other,
    wd_other,
    layer_out,
    residual_out,
    slab_out,
    slots,
    sums,
    gates,
    ups,
    downs,
    actives,
    grad_gates,
    grad_ups,
    far_y,
    near_y,
    far_z,
    near_z,
    packed,
    returned,
    load_sem,
    send,
    recv,
):
    net = Net(send, recv)
    loads = []
    for half, sources in enumerate(((wg_ref, wu_ref, wd_ref), (wg_other, wu_other, wd_other))):
        for i, (source, target) in enumerate(zip(sources, (gates, ups, downs))):
            made = pltpu.make_async_copy(source, target.at[half], load_sem.at[half * 3 + i])
            made.start()
            loads.append(made)
    net.barrier(net.ring_devices() + net.peer_devices())

    for quarter in range(4):
        rows = jnp.dot(packing(quarter, False), arrived_ref[...], preferred_element_type=F32)
        rows = rows.astype(BF16)
        for e in range(2):
            slots[e, 0:ROWS, quarter * CHUNK : (quarter + 1) * CHUNK] = rows[e * 16 : e * 16 + 16]

    def block(ref, e):
        full = lambda r: ref.at[e, pl.ds(r * ROWS, ROWS), :]
        half = lambda r, h: ref.at[e, pl.ds(r * ROWS, ROWS), pl.ds(h * D, D)]
        return full, half

    gather = [gather_steps(net, *block(slots, e), lambda r: None) for e in range(2)]
    reduce = [
        reduce_steps(
            net,
            *block(sums, e),
            [near_y.at[e, 0], near_y.at[e, 1], near_z.at[e, 0], near_z.at[e, 1]],
            [far_y.at[e, 0], far_y.at[e, 1], far_z.at[e, 0], far_z.at[e, 1]],
            load_wide,
            store_narrow,
        )
        for e in range(2)
    ]

    def compute_steps(e):
        def enter(half):
            inputs = slots[e, :, :D]
            gate = lax.dot_general(inputs, gates[half, e], NT, preferred_element_type=F32)
            up = lax.dot_general(inputs, ups[half, e], NT, preferred_element_type=F32)
            grad = lax.dot_general(
                slots[e, :, D:], downs[half, e], NT, preferred_element_type=F32
            )
            s = jax.nn.sigmoid(gate)
            swish = gate * s
            actives[half] = (swish * up).astype(BF16)
            grad_gates[half] = (grad * up * s * (1.0 + gate * (1.0 - s))).astype(BF16)
            grad_ups[half] = (grad * swish).astype(BF16)

        def leave(n):
            columns = pl.ds(n * 512, 512)
            total = jnp.zeros((CHIP_ROWS, 512), F32)
            for half in range(2):
                total = total + jnp.dot(
                    actives[half], downs[half, e, :, columns], preferred_element_type=F32
                )
            sums[e, :, pl.ds(n * 512, 512)] = total.astype(BF16)

        def leave_grad(n):
            columns = pl.ds(n * 512, 512)
            total = jnp.zeros((CHIP_ROWS, 512), F32)
            for half in range(2):
                total = total + jnp.dot(
                    grad_gates[half], gates[half, e, :, columns], preferred_element_type=F32
                )
                total = total + jnp.dot(
                    grad_ups[half], ups[half, e, :, columns], preferred_element_type=F32
                )
            sums[e, :, pl.ds(D + n * 512, 512)] = total.astype(BF16)

        steps = [lambda half=half: enter(half) for half in range(2)]
        steps += [lambda n=n: leave(n) for n in range(4)]
        steps += [lambda n=n: leave_grad(n) for n in range(4)]
        return steps

    (first0, relays0, last0), (first1, relays1, last1) = gather
    (start0, rest0), (start1, rest1) = reduce
    for step in first0 + relays0 + first1 + last0:
        step()
    for made in loads:
        made.wait()
    merge(relays1, compute_steps(0))
    for step in start0 + last1:
        step()
    compute1 = compute_steps(1)
    merge(rest0[:4], compute1)
    for step in start1:
        step()
    merge(rest0[4:], rest1[:4])
    for step in rest1[4:]:
        step()

    def piece(ref, peer):
        return ref.at[pl.ds(pl.multiple_of(peer * ROWS, ROWS), ROWS), :]

    me = net.exp
    spread = jnp.zeros((128, CHUNK), F32)
    for quarter in range(4):
        columns = slice(quarter * CHUNK, (quarter + 1) * CHUNK)
        both = jnp.concatenate((sums[0, 0:ROWS, columns], sums[1, 0:ROWS, columns]), axis=0)
        spread = spread + jnp.dot(packing(quarter, True), both, preferred_element_type=F32)
    packed[...] = spread.astype(BF16)
    moved = net.push(lambda peer: piece(packed, peer), piece(returned, me))
    piece(returned, me)[...] = piece(packed, me)[...]
    found = places(ids_ref)
    weight = [column(gw_ref, k) for k in range(2)]
    wide = hidden_ref[...].astype(F32)
    inverse_norm = lax.rsqrt(jnp.mean(wide * wide, axis=1, keepdims=True) + EPSILON)
    for made in moved:
        made.wait_recv()

    def pick(k, quarter):
        return jnp.dot(one_hot(found[k], quarter), returned[...], preferred_element_type=F32)

    for quarter in range(2):
        columns = slice(quarter * CHUNK, (quarter + 1) * CHUNK)
        mixture = weight[0] * pick(0, quarter) + weight[1] * pick(1, quarter)
        layer_out[:, columns] = (wide[:, columns] + mixture).astype(BF16)
    grad_normed = jnp.concatenate([pick(0, q) + pick(1, q) for q in (2, 3)], axis=1)
    scaled = gain_ref[...] * grad_normed
    cube = inverse_norm * inverse_norm * inverse_norm
    grad_hidden = go_ref[...].astype(F32) + (
        inverse_norm * scaled
        - wide * cube * jnp.mean(wide * scaled, axis=1, keepdims=True)
    )
    residual_out[...] = grad_hidden.astype(BF16)
    piece(slab_out, me)[...] = residual_out[...]
    moved = net.push(lambda peer: residual_out, piece(slab_out, me))
    for made in moved:
        made.wait_recv()
    net.finish()


def backward_kernel(
    slab_ref,
    ow_ref,
    q_ref,
    kv_ref,
    p_ref,
    att_ref,
    pairs,
    grads,
    grad_heads,
    sums,
    dq_rows,
    dq_other,
    far_y,
    near_y,
    far_z,
    near_z,
    send,
    recv,
):
    net = Net(send, recv)
    core = net.core
    own_rows = pl.ds(pl.multiple_of(core * 128, 128), 128)
    other_rows = pl.ds(pl.multiple_of((1 - core) * 128, 128), 128)
    own_values = pl.ds(pl.multiple_of(256 + core * 128, 128), 128)
    other_values = pl.ds(pl.multiple_of(256 + (1 - core) * 128, 128), 128)
    net.barrier(net.ring_devices() + [net.sibling])
    for head in range(2):
        grads[head] = lax.dot_general(
            slab_ref[...], ow_ref[head * 128 : head * 128 + 128, :], NT, preferred_element_type=F32
        ).astype(BF16)
    swap = net.copy(grads.at[1 - core], grad_heads.at[own_rows, :], net.sibling)
    grad_heads[own_rows, :] = grads[core]
    swap.wait_recv()
    grad_head = grad_heads[...]
    delta = jnp.sum(grad_head.astype(F32) * att_ref[...].astype(F32), axis=1, keepdims=True)

    dq_rows[...] = jnp.zeros((CHIP_ROWS, HD), F32)

    def block(r):
        low = p_ref[r]
        grad_prob = lax.dot_general(grad_head, kv_ref[r, 256:, :], NT, preferred_element_type=F32)
        grad_score = (low.astype(F32) * (grad_prob - delta)).astype(BF16)
        dq_rows[...] += jnp.dot(grad_score, kv_ref[r, :256, :], preferred_element_type=F32)
        sums[r, :256, :] = (
            lax.dot_general(grad_score, q_ref[...], TN, preferred_element_type=F32) * SCALE
        ).astype(BF16)
        sums[r, 256:, :] = lax.dot_general(
            low, grad_head, TN, preferred_element_type=F32
        ).astype(BF16)

    start, rest = reduce_steps(
        net,
        lambda r: sums.at[r],
        lambda r, h: sums.at[r, pl.ds(h * 256, 256), :],
        [near_y.at[0], near_y.at[1], near_z.at[0], near_z.at[1]],
        [far_y.at[0], far_y.at[1], far_z.at[0], far_z.at[1]],
        load_wide,
        store_narrow,
    )
    order = (2, 1, 3, 0)
    for dz, step in zip(order, start):
        block(rel(2, dz))
        step()
    for dz, step in zip(order, rest[:4]):
        block(rel(1, dz))
        block(rel(3, dz))
        step()
    for dz in order:
        block(rel(0, dz))
    dq_other[...] = (dq_rows[other_rows, :] * SCALE).astype(BF16)
    swaps = [net.copy(dq_other, pairs.at[0, core], net.sibling)]
    pairs[0, core] = (dq_rows[own_rows, :] * SCALE).astype(BF16)
    for step in rest[4:]:
        step()
    swaps.append(net.copy(sums.at[0, other_rows, :], pairs.at[1, core], net.sibling))
    swaps.append(net.copy(sums.at[0, other_values, :], pairs.at[2, core], net.sibling))
    pairs[1, core] = sums[0, own_rows, :]
    pairs[2, core] = sums[0, own_values, :]
    for made in swaps:
        made.wait_recv()
    net.finish()


def finish_kernel(pairs, layer_ref, residual_ref, layer_out, residual_out, *outs):
    layer_out[...] = layer_ref[...]
    residual_out[...] = residual_ref[...]
    for i, out in enumerate(outs):
        out[:, :128] = pairs[i, 0]
        out[:, 128:] = pairs[i, 1]


def call(kernel, collective_id, outs, ins, scratch, copies, flops):
    shapes, out_specs = zip(*outs)
    args, in_specs = zip(*ins)
    spec = {"vmem": pl.BlockSpec(memory_space=pltpu.VMEM), "any": pl.BlockSpec(memory_space=pl.ANY)}
    return pl.pallas_call(
        kernel,
        out_shape=[jax.ShapeDtypeStruct(*shape) for shape in shapes],
        in_specs=[spec[s] for s in in_specs],
        out_specs=[spec[s] for s in out_specs],
        scratch_shapes=list(scratch)
        + [pltpu.SemaphoreType.DMA((copies,)), pltpu.SemaphoreType.DMA((copies,))],
        compiler_params=pltpu.CompilerParams(
            collective_id=collective_id, has_side_effects=True, vmem_limit_bytes=VMEM_LIMIT
        ),
        cost_estimate=pl.CostEstimate(flops=flops, bytes_accessed=1 << 24, transcendentals=0),
    )(*args)


def local(
    residual,
    query_states,
    key_states,
    value_states,
    out_weight,
    norm_gain,
    expert_ids,
    gate_weights,
    gate_matrix,
    up_matrix,
    down_matrix,
    grad_out,
):
    gain = norm_gain.reshape(1, D)
    expert_ids, gate_weights = expert_ids.T, gate_weights.T
    gate_matrix = gate_matrix.transpose(0, 2, 1)
    up_matrix = up_matrix.transpose(0, 2, 1)
    vm = lambda *args: [(arg, "vmem") for arg in args]
    hbm = lambda *args: [(arg, "any") for arg in args]
    like = lambda arg: ((arg.shape, arg.dtype), "any")
    out = lambda *shape: ((shape, BF16), "vmem")
    v = lambda *shape: pltpu.VMEM(shape, BF16)
    queries, keys_values, softmax, attended, hidden, arrived, wg, wu, wd = call(
        forward_kernel,
        0,
        [
            out(CHIP_ROWS, HD),
            out(CHIPS, 512, HD),
            out(CHIPS, CHIP_ROWS, CHIP_ROWS),
            out(CHIP_ROWS, HD),
            out(ROWS, D),
            out(128, CHUNK),
            like(gate_matrix),
            like(up_matrix),
            like(down_matrix),
        ],
        vm(
            query_states,
            key_states,
            value_states,
            out_weight,
            residual,
            gain,
            expert_ids,
            gate_weights,
            grad_out,
        )
        + hbm(gate_matrix, up_matrix, down_matrix),
        [
            pltpu.VMEM((CHIPS, CHIP_ROWS, CHIP_ROWS), F32),
            v(2, 128, HD),
            v(128, D),
            v(128, D),
            v(128, CHUNK),
        ],
        41,
        10**9,
    )
    layer_out, grad_residual, slab = call(
        expert_kernel,
        1,
        [out(ROWS, D), out(ROWS, D), out(128, D)],
        vm(arrived, hidden, gain, expert_ids, gate_weights, grad_out)
        + hbm(gate_matrix, up_matrix, down_matrix, wg, wu, wd),
        [
            v(2, CHIP_ROWS, 2 * D),
            v(2, CHIP_ROWS, 2 * D),
            v(2, 2, HIDDEN, D),
            v(2, 2, HIDDEN, D),
            v(2, 2, HIDDEN, D),
            v(2, CHIP_ROWS, HIDDEN),
            v(2, CHIP_ROWS, HIDDEN),
            v(2, CHIP_ROWS, HIDDEN),
            v(2, 2, 4, ROWS, D),
            v(2, 2, 4, ROWS, 2 * D),
            v(2, 2, ROWS, D),
            v(2, 2, ROWS, 2 * D),
            v(128, CHUNK),
            v(128, CHUNK),
            pltpu.SemaphoreType.DMA((6,)),
        ],
        94,
        5 * 10**9,
    )
    (pairs,) = call(
        backward_kernel,
        2,
        [out(3, 2, 128, HD)],
        vm(slab, out_weight, queries, keys_values, softmax, attended),
        [
            v(2, 128, HD),
            v(CHIP_ROWS, HD),
            v(CHIPS, 512, HD),
            pltpu.VMEM((CHIP_ROWS, HD), F32),
            v(128, HD),
            v(2, 4, 256, HD),
            v(2, 4, 512, HD),
            v(2, 256, HD),
            v(2, 512, HD),
        ],
        24,
        2 * 10**9,
    )
    shapes = [(ROWS, D)] * 2 + [(128, 2 * HD)] * 3
    return pl.pallas_call(
        finish_kernel,
        out_shape=[jax.ShapeDtypeStruct(shape, BF16) for shape in shapes],
    )(pairs, layer_out, grad_residual)


def solution(mesh):
    in_specs = (
        P(("ctx", "exp"), None),
        P("ctx", "exp"),
        P("ctx", "exp"),
        P("ctx", "exp"),
        P("exp", None),
        P(),
        P(("ctx", "exp"), None),
        P(("ctx", "exp"), None),
        P("exp", None, "ctx"),
        P("exp", None, "ctx"),
        P("exp", "ctx", None),
        P(("ctx", "exp"), None),
    )
    out_specs = (
        P(("ctx", "exp"), None),
        P(("ctx", "exp"), None),
        P("ctx", "exp"),
        P("ctx", "exp"),
        P("ctx", "exp"),
    )
    return jax.shard_map(local, mesh=mesh, in_specs=in_specs, out_specs=out_specs, check_vma=False)
```

```python
import math

import jax
import jax.numpy as jnp
from jax import lax
from jax.experimental import pallas as pl
from jax.experimental.pallas import tpu as pltpu
from jax.sharding import PartitionSpec as P

MESH = pl.DeviceIdType.MESH
F32 = jnp.float32
BF16 = jnp.bfloat16
HD = 128
D = 2048
ROWS = 16
CHIPS = 16
N_EXP = 8
CHIP_ROWS = 256
HIDDEN = 200
CHUNK = 1024
EPSILON = 1e-05
MASKED = -1e30
SCALE = 1.0 / math.sqrt(HD)
VMEM_LIMIT = 58 * 1024 * 1024
COPIES = 260

ATTENTION_ORDER = (
    0, 1, 36, 17, 16, 2, 18, 37, 3, 4, 19, 20, 5, 21, 6, 22, 9, 11, 24, 25, 8, 7, 23, 12, 27, 10,
    32, 28, 26, 35, 33, 34,
)
EXPERT_ORDER = (
    0, 33, 1, 32, 16, 17, 49, 34, 4, 48, 50, 2, 35, 36, 3, 18, 19, 20, 5, 6, 38, 37, 7, 51, 9, 22,
    40, 52, 21, 12, 41, 11, 8, 43, 10, 128, 129, 53, 55, 54, 133, 135, 25, 134, 132, 64, 65, 44, 39,
    42, 144, 67, 24, 23, 27, 145, 28, 149, 57, 66, 150, 151, 26, 130, 148, 96, 68, 131, 139, 60, 73,
    97, 56, 59, 58, 136, 137, 98, 138, 80, 146, 147, 81, 69, 153, 71, 100, 155, 152, 154, 113, 112,
    101, 84, 103, 116, 114, 99, 83, 104, 115, 72, 75, 74, 119, 85, 87, 82, 106, 117, 105, 120, 107,
    89, 121, 70, 102, 123, 122, 88, 86, 91, 90, 76, 118, 77, 108, 92, 109, 124, 125, 93,
)
BACKWARD_ORDER = (
    42, 1, 43, 41, 0, 46, 38, 17, 45, 4, 34, 16, 37, 2, 39, 20, 47, 32, 40, 7, 3, 35, 18, 23, 19,
    33, 8, 44, 9, 10, 11, 21, 24, 5, 36, 25, 26, 27, 22, 6, 48, 12, 28, 13, 29,
)
NT = (((1,), (1,)), ((), ()))
TN = (((0,), (0,)), ((), ()))


def rel(dy, dz):
    return dy * 4 + dz


class Net:
    def __init__(self, send, recv):
        self.send, self.recv, self.count, self.started = send, recv, 0, []
        ctx = lax.axis_index("ctx")
        self.exp = lax.axis_index("exp")
        self.core = lax.rem(ctx, 2)
        chip = ctx // 2
        self.y, self.z = chip // 4, lax.rem(chip, 4)
        at = lambda y, z, c: {"ctx": (lax.rem(y, 4) * 4 + lax.rem(z, 4)) * 2 + c}
        self.yp = at(self.y + 1, self.z, self.core)
        self.ym = at(self.y + 3, self.z, self.core)
        self.zp = at(self.y, self.z + 1, self.core)
        self.zm = at(self.y, self.z + 3, self.core)
        self.sibling = at(self.y, self.z, 1 - self.core)
        self.peers = [lax.rem(self.exp + d, N_EXP) for d in range(1, N_EXP)]

    def copy(self, src, dst, device):
        i = self.count
        self.count += 1
        made = pltpu.make_async_remote_copy(
            src_ref=src,
            dst_ref=dst,
            send_sem=self.send.at[i],
            recv_sem=self.recv.at[i],
            device_id=device,
            device_id_type=MESH,
        )
        made.start()
        self.started.append(made)
        return made

    def finish(self):
        for made in self.started:
            made.wait_send()

    def barrier(self, devices):
        sem = pltpu.get_barrier_semaphore()
        for device in devices:
            pl.semaphore_signal(sem, inc=1, device_id=device, device_id_type=MESH)
        pl.semaphore_wait(sem, len(devices))

    def ring_devices(self):
        return [self.yp, self.ym, self.zp, self.zm]

    def peer_devices(self):
        return [{"exp": peer} for peer in self.peers]

    def push(self, src_of, dst):
        return [self.copy(src_of(peer), dst, {"exp": peer}) for peer in self.peers]


def gather_steps(net, full, half, seen=lambda r: None):
    state = {}

    def send_z():
        state["z3"] = net.copy(full(rel(0, 0)), full(rel(0, 3)), net.zp)
        state["z1"] = net.copy(full(rel(0, 0)), full(rel(0, 1)), net.zm)

    def send_y(dz):
        state["y3", dz] = net.copy(full(rel(0, dz)), full(rel(3, dz)), net.yp)
        state["y1", dz] = net.copy(full(rel(0, dz)), full(rel(1, dz)), net.ym)

    def near_z3():
        state["z3"].wait_recv()
        state["h0"] = net.copy(half(rel(0, 3), 0), half(rel(0, 2), 0), net.zp)
        send_y(3)
        seen(rel(0, 3))

    def near_z1():
        state["z1"].wait_recv()
        state["h1"] = net.copy(half(rel(0, 1), 1), half(rel(0, 2), 1), net.zm)
        send_y(1)
        seen(rel(0, 1))

    def far_z():
        state["h0"].wait_recv()
        state["h1"].wait_recv()
        send_y(2)
        seen(rel(0, 2))

    def near_y(dz):
        state["y3", dz].wait_recv()
        state["y1", dz].wait_recv()
        if dz in (0, 2):
            state["g0", dz] = net.copy(half(rel(3, dz), 0), half(rel(2, dz), 0), net.yp)
            state["g1", dz] = net.copy(half(rel(1, dz), 1), half(rel(2, dz), 1), net.ym)
        seen(rel(3, dz))
        seen(rel(1, dz))

    def far_y(dz):
        state["g0", dz].wait_recv()
        state["g1", dz].wait_recv()
        if dz == 0:
            state["f3"] = net.copy(full(rel(2, 0)), full(rel(2, 3)), net.zp)
            state["f1"] = net.copy(full(rel(2, 0)), full(rel(2, 1)), net.zm)
        seen(rel(2, dz))

    def end(dz):
        state["f%d" % dz].wait_recv()
        seen(rel(2, dz))

    return [
        send_z,
        lambda: send_y(0),
        lambda: near_y(0),
        near_z3,
        near_z1,
        lambda: far_y(0),
        far_z,
        lambda: near_y(3),
        lambda: near_y(1),
        lambda: near_y(2),
        lambda: far_y(2),
        lambda: end(3),
        lambda: end(1),
    ]


def reduce_steps(net, full, half, far_y, near_y, far_z, near_z):
    ra, rb, za, zb = far_y.at[0], far_y.at[1], far_z.at[0], far_z.at[1]
    rc, rd = near_y.at[0], near_y.at[1]
    zc, zd, ze, zf = [near_z.at[i] for i in range(4)]
    state = {}

    def add(target, *sources):
        total = target[...].astype(F32)
        for source in sources:
            total = total + source[...].astype(F32)
        target[...] = total.astype(BF16)

    def send_far_z():
        state["e"] = net.copy(full(rel(2, 1)), ze, net.zp)
        state["f"] = net.copy(full(rel(2, 3)), zf, net.zm)

    def send_far_y(dz):
        if dz == 0:
            state["e"].wait_recv()
            state["f"].wait_recv()
            add(full(rel(2, 0)), ze, zf)
        state["a", dz] = net.copy(half(rel(2, dz), 0), ra.at[dz // 2], net.yp)
        state["b", dz] = net.copy(half(rel(2, dz), 1), rb.at[dz // 2], net.ym)

    def send_near(dz):
        if dz in (0, 2):
            state["a", dz].wait_recv()
            state["b", dz].wait_recv()
            add(half(rel(1, dz), 0), ra.at[dz // 2])
            add(half(rel(3, dz), 1), rb.at[dz // 2])
        state["c", dz] = net.copy(full(rel(1, dz)), rc.at[dz], net.yp)
        state["d", dz] = net.copy(full(rel(3, dz)), rd.at[dz], net.ym)

    def collect(dz):
        state["c", dz].wait_recv()
        state["d", dz].wait_recv()
        add(full(rel(0, dz)), rc.at[dz], rd.at[dz])
        if dz == 2:
            state["za"] = net.copy(half(rel(0, 2), 0), za, net.zp)
            state["zb"] = net.copy(half(rel(0, 2), 1), zb, net.zm)

    def send_z1():
        state["za"].wait_recv()
        add(half(rel(0, 1), 0), za)
        state["zc"] = net.copy(full(rel(0, 1)), zc, net.zp)

    def send_z3():
        state["zb"].wait_recv()
        add(half(rel(0, 3), 1), zb)
        state["zd"] = net.copy(full(rel(0, 3)), zd, net.zm)

    def last():
        state["zc"].wait_recv()
        state["zd"].wait_recv()
        add(full(rel(0, 0)), zc, zd)

    return [
        send_far_z,
        lambda: send_far_y(2),
        lambda: send_near(1),
        lambda: send_near(3),
        lambda: send_near(2),
        lambda: send_far_y(0),
        lambda: send_near(0),
        lambda: collect(2),
        lambda: collect(1),
        lambda: collect(3),
        send_z1,
        send_z3,
        lambda: collect(0),
        last,
    ]


def run(order, parts):
    assert sorted(order) == [16 * p + s for p, part in enumerate(parts) for s in range(len(part))]
    for code in order:
        parts[code // 16][code % 16]()


def column(ref, k):
    diagonal = lax.broadcasted_iota(jnp.int32, (ROWS, ROWS), 0) == lax.broadcasted_iota(
        jnp.int32, (ROWS, ROWS), 1
    )
    row = jnp.broadcast_to(ref[k : k + 1, :], (ROWS, ROWS))
    return jnp.sum(jnp.where(diagonal, row, jnp.zeros_like(row)), axis=1, keepdims=True)


def places(ids_ref):
    lanes = lax.broadcasted_iota(jnp.int32, (ROWS, 128), 1)
    ids = [column(ids_ref, k) for k in range(2)]
    chosen = [(lanes == one).astype(F32) for one in ids]
    lower = (
        lax.broadcasted_iota(jnp.int32, (ROWS, ROWS), 1)
        < lax.broadcasted_iota(jnp.int32, (ROWS, ROWS), 0)
    ).astype(BF16)
    earlier = jnp.dot(lower, (chosen[0] + chosen[1]).astype(BF16), preferred_element_type=F32)
    found = []
    for one, hot in zip(ids, chosen):
        rank = jnp.sum(earlier * hot, axis=1, keepdims=True).astype(jnp.int32)
        place = (one >> 1) * 16 + (one & 1) * 2 + rank
        found.append(jnp.where(rank < 2, place, -1000))
    return found


def one_hot(place, quarter):
    lanes = lax.broadcasted_iota(jnp.int32, (ROWS, 128), 1)
    return (lanes == place + 4 * quarter).astype(BF16)


def packing(quarter, transposed):
    shape, slot_dim = ((128, 32), 1) if transposed else ((32, 128), 0)
    slot = lax.broadcasted_iota(jnp.int32, shape, slot_dim)
    packed = lax.broadcasted_iota(jnp.int32, shape, 1 - slot_dim)
    want = ((slot & 15) >> 1) * 16 + quarter * 4 + (slot >> 4) * 2 + (slot & 1)
    return (packed == want).astype(BF16)


def layer_kernel(
    q_ref,
    k_ref,
    v_ref,
    residual_ref,
    gain_ref,
    ids_ref,
    gw_ref,
    go_ref,
    ow_hbm,
    wg_hbm,
    wu_hbm,
    wd_hbm,
    layer_out,
    residual_out,
    pairs,
    ow_ref,
    queries,
    kv,
    softmax,
    attended_rows,
    scores,
    row_top,
    row_sum,
    att_pair,
    partial,
    pieces,
    packed,
    arrived,
    slots,
    sums,
    gates,
    ups,
    downs,
    gate_part,
    up_part,
    actives,
    grad_gates,
    grad_ups,
    far_y,
    near_y,
    far_z,
    near_z,
    packed_back,
    returned,
    slab,
    grads,
    grad_heads,
    grad_sums,
    dq_rows,
    dq_other,
    att_far_y,
    att_near_y,
    att_far_z,
    att_near_z,
    load_sem,
    send,
    recv,
):
    net = Net(send, recv)
    core, me = net.core, net.exp
    own_rows = pl.ds(pl.multiple_of(core * 128, 128), 128)
    other_rows = pl.ds(pl.multiple_of((1 - core) * 128, 128), 128)
    own_values = pl.ds(pl.multiple_of(256 + core * 128, 128), 128)
    other_values = pl.ds(pl.multiple_of(256 + (1 - core) * 128, 128), 128)

    def piece(ref, peer):
        return ref.at[pl.ds(pl.multiple_of(peer * ROWS, ROWS), ROWS), :]

    def mine(ref):
        return jnp.where(core == 0, ref[:, :128], ref[:, 128:])

    weights = ((wg_hbm, gates), (wu_hbm, ups), (wd_hbm, downs))
    loads = [pltpu.make_async_copy(ow_hbm, ow_ref, load_sem.at[0])]
    for i, (source, target) in enumerate(weights):
        loads.append(pltpu.make_async_copy(source, target.at[0], load_sem.at[i + 1]))
    for made in loads:
        made.start()
    net.barrier(net.ring_devices() + [net.sibling] + net.peer_devices())

    exchange = [
        net.copy(k_ref.at[:, other_rows], kv.at[0, own_rows, :], net.sibling),
        net.copy(q_ref.at[:, other_rows], queries.at[own_rows, :], net.sibling),
        net.copy(v_ref.at[:, other_rows], kv.at[0, own_values, :], net.sibling),
    ]
    kv[0, own_rows, :] = mine(k_ref)
    kv[0, own_values, :] = mine(v_ref)
    queries[own_rows, :] = mine(q_ref)

    chip = net.y * 4 + net.z

    def score_block(r):
        dy, dz = r // 4, r % 4
        other = lax.rem(net.y + dy, 4) * 4 + lax.rem(net.z + dz, 4)
        s = lax.dot_general(queries[...], kv[r, :256, :], NT, preferred_element_type=F32) * SCALE
        row = lax.broadcasted_iota(jnp.int32, (CHIP_ROWS, CHIP_ROWS), 0) + chip * CHIP_ROWS
        place = lax.broadcasted_iota(jnp.int32, (CHIP_ROWS, CHIP_ROWS), 1) + other * CHIP_ROWS
        s = jnp.where(place <= row, s, MASKED)
        scores[r] = s
        row_top[...] = jnp.maximum(row_top[...], jnp.maximum(s[:, :128], s[:, 128:]))

    row_top[...] = jnp.full((CHIP_ROWS, 128), MASKED, F32)
    row_sum[...] = jnp.zeros((CHIP_ROWS, 128), F32)

    def raise_blocks(quarter):
        m = jnp.max(row_top[...], axis=1, keepdims=True)

        def one(r, total):
            e = jnp.exp(scores[r] - m)
            scores[r] = e
            return total + (e[:, :128] + e[:, 128:])

        row_sum[...] = lax.fori_loop(4 * quarter, 4 * quarter + 4, one, row_sum[...])

    def pair(ref, start, seen):
        full = lambda r: ref.at[r, pl.ds(start, 256), :]
        half = lambda r, h: ref.at[r, pl.ds(start + h * 128, 128), :]
        return gather_steps(net, full, half, seen)

    raises = [lambda i=i: raise_blocks(i) for i in range(4)]
    for made in exchange:
        made.wait_recv()
    other_weights = []

    def send_weights():
        for source, target in weights:
            other_weights.append(net.copy(source, target.at[1], net.sibling))

    attention = [
        pair(kv, 0, score_block),
        pair(kv, 256, lambda r: None),
        raises + [lambda: score_block(0), send_weights],
    ]
    run(ATTENTION_ORDER, attention)
    inverse = 1.0 / jnp.sum(row_sum[...], axis=1, keepdims=True)

    def attend(r, acc):
        low = (scores[r] * inverse).astype(BF16)
        softmax[r] = low
        return acc + jnp.dot(low, kv[r, 256:, :], preferred_element_type=F32)

    attended = lax.fori_loop(0, CHIPS, attend, jnp.zeros((CHIP_ROWS, HD), F32))
    attended_rows[...] = attended.astype(BF16)
    swap = net.copy(attended_rows.at[other_rows, :], att_pair.at[core], net.sibling)
    att_pair[core] = attended_rows[own_rows, :]
    for made in loads:
        made.wait()
    swap.wait_recv()

    for n in range(4):
        columns = pl.ds(n * 512, 512)
        partial[:, columns] = (
            jnp.dot(att_pair[0], ow_ref[:128, columns], preferred_element_type=F32)
            + jnp.dot(att_pair[1], ow_ref[128:, columns], preferred_element_type=F32)
        ).astype(BF16)
    moved = net.push(lambda peer: piece(partial, peer), piece(pieces, me))
    piece(pieces, me)[...] = piece(partial, me)[...]
    found = places(ids_ref)
    weight = [column(gw_ref, k) for k in range(2)]
    grad_out = go_ref[...].astype(F32)
    weighted = [(weight[k] * grad_out).astype(BF16) for k in range(2)]
    for made in moved:
        made.wait_recv()
    projected = pieces[0:ROWS, :].astype(F32)
    for j in range(1, N_EXP):
        projected = projected + pieces[j * ROWS : (j + 1) * ROWS, :].astype(F32)
    wide = (residual_ref[...].astype(F32) + projected).astype(BF16).astype(F32)
    inverse_norm = lax.rsqrt(jnp.mean(wide * wide, axis=1, keepdims=True) + EPSILON)
    normed = (wide * inverse_norm * gain_ref[...]).astype(BF16)
    spread = jnp.zeros((128, CHUNK), F32)
    for quarter in range(4):
        for k in range(2):
            source = normed if quarter < 2 else weighted[k]
            low = (quarter % 2) * CHUNK
            spread = spread + lax.dot_general(
                one_hot(found[k], quarter),
                source[:, low : low + CHUNK],
                TN,
                preferred_element_type=F32,
            )
    packed[...] = spread.astype(BF16)
    moved = net.push(lambda peer: piece(packed, peer), piece(arrived, me))
    piece(arrived, me)[...] = piece(packed, me)[...]
    for made in moved:
        made.wait_recv()
    for quarter in range(4):
        rows = jnp.dot(packing(quarter, False), arrived[...], preferred_element_type=F32)
        rows = rows.astype(BF16)
        for e in range(2):
            slots[e, 0:ROWS, quarter * CHUNK : (quarter + 1) * CHUNK] = rows[e * 16 : e * 16 + 16]

    def block(ref, e, part):
        full = lambda r: ref.at[e, pl.ds(r * ROWS, ROWS), pl.ds(part * D, D)]
        half = lambda r, h: ref.at[
            e, pl.ds(r * ROWS, ROWS), pl.ds(part * D + h * CHUNK, CHUNK)
        ]
        return full, half

    parts = [(e, part) for e in range(2) for part in range(2)]
    experts = [gather_steps(net, *block(slots, e, part)) for e, part in parts]
    for i, (e, part) in enumerate(parts):
        buffers = [ref.at[i] for ref in (far_y, near_y, far_z, near_z)]
        experts.append(reduce_steps(net, *block(sums, e, part), *buffers))

    def compute_steps(e):
        def enter(half):
            inputs = slots[e, :, :D]
            gate = lax.dot_general(inputs, gates[half, e], NT, preferred_element_type=F32)
            up = lax.dot_general(inputs, ups[half, e], NT, preferred_element_type=F32)
            gate_part[e, half] = gate
            up_part[e, half] = up
            actives[e, half] = (gate * jax.nn.sigmoid(gate) * up).astype(BF16)

        def enter_grad(half):
            grad = lax.dot_general(
                slots[e, :, D:], downs[half, e], NT, preferred_element_type=F32
            )
            gate, up = gate_part[e, half], up_part[e, half]
            s = jax.nn.sigmoid(gate)
            grad_gates[e, half] = (grad * up * s * (1.0 + gate * (1.0 - s))).astype(BF16)
            grad_ups[e, half] = (grad * gate * s).astype(BF16)

        def leave(n, start, terms):
            columns = pl.ds(n * 512, 512)
            total = jnp.zeros((CHIP_ROWS, 512), F32)
            for half in range(2):
                for rows, matrix in terms:
                    total = total + jnp.dot(
                        rows[e, half], matrix[half, e, :, columns], preferred_element_type=F32
                    )
            sums[e, :, pl.ds(start + n * 512, 512)] = total.astype(BF16)

        out_terms = [(actives, downs)]
        grad_terms = [(grad_gates, gates), (grad_ups, ups)]
        steps = [lambda half=half: enter(half) for half in range(2)]
        steps += [lambda half=half: enter_grad(half) for half in range(2)]
        steps += [lambda n=n: leave(n, 0, out_terms) for n in range(4)]
        steps += [lambda n=n: leave(n, D, grad_terms) for n in range(4)]
        return steps

    experts += [compute_steps(e) for e in range(2)]
    for made in other_weights:
        made.wait_recv()
    run(EXPERT_ORDER, experts)

    spread = jnp.zeros((128, CHUNK), F32)
    for quarter in range(4):
        columns = slice(quarter * CHUNK, (quarter + 1) * CHUNK)
        both = jnp.concatenate((sums[0, 0:ROWS, columns], sums[1, 0:ROWS, columns]), axis=0)
        spread = spread + jnp.dot(packing(quarter, True), both, preferred_element_type=F32)
    packed_back[...] = spread.astype(BF16)
    moved = net.push(lambda peer: piece(packed_back, peer), piece(returned, me))
    piece(returned, me)[...] = piece(packed_back, me)[...]
    for made in moved:
        made.wait_recv()

    def pick(k, quarter):
        return jnp.dot(one_hot(found[k], quarter), returned[...], preferred_element_type=F32)

    grad_normed = jnp.concatenate([pick(0, q) + pick(1, q) for q in (2, 3)], axis=1)
    scaled = gain_ref[...] * grad_normed
    cube = inverse_norm * inverse_norm * inverse_norm
    grad_hidden = grad_out + (
        inverse_norm * scaled - wide * cube * jnp.mean(wide * scaled, axis=1, keepdims=True)
    )
    residual_out[...] = grad_hidden.astype(BF16)
    moved = net.push(lambda peer: residual_out, piece(slab, me))
    piece(slab, me)[...] = residual_out[...]
    for quarter in range(2):
        columns = slice(quarter * CHUNK, (quarter + 1) * CHUNK)
        mixture = weight[0] * pick(0, quarter) + weight[1] * pick(1, quarter)
        layer_out[:, columns] = (wide[:, columns] + mixture).astype(BF16)
    for made in moved:
        made.wait_recv()

    for head in range(2):
        grads[head] = lax.dot_general(
            slab[...], ow_ref[head * 128 : head * 128 + 128, :], NT, preferred_element_type=F32
        ).astype(BF16)
    swap = net.copy(grads.at[1 - core], grad_heads.at[own_rows, :], net.sibling)
    grad_heads[own_rows, :] = grads[core]
    swap.wait_recv()
    grad_head = grad_heads[...]
    delta = jnp.sum(
        grad_head.astype(F32) * attended_rows[...].astype(F32), axis=1, keepdims=True
    )
    dq_rows[...] = jnp.zeros((CHIP_ROWS, HD), F32)

    def back(r):
        low = softmax[r]
        grad_prob = lax.dot_general(grad_head, kv[r, 256:, :], NT, preferred_element_type=F32)
        grad_score = (low.astype(F32) * (grad_prob - delta)).astype(BF16)
        dq_rows[...] += jnp.dot(grad_score, kv[r, :256, :], preferred_element_type=F32)
        grad_sums[r, :256, :] = (
            lax.dot_general(grad_score, queries[...], TN, preferred_element_type=F32) * SCALE
        ).astype(BF16)
        grad_sums[r, 256:, :] = lax.dot_general(
            low, grad_head, TN, preferred_element_type=F32
        ).astype(BF16)

    swaps = []

    def send_queries():
        dq_other[...] = (dq_rows[other_rows, :] * SCALE).astype(BF16)
        swaps.append(net.copy(dq_other, pairs.at[0, core], net.sibling))
        pairs[0, core] = (dq_rows[own_rows, :] * SCALE).astype(BF16)

    def key_sums(i):
        full = lambda r: grad_sums.at[r, pl.ds(i * 256, 256), :]
        half = lambda r, h: grad_sums.at[r, pl.ds(i * 256 + h * 128, 128), :]
        return reduce_steps(
            net,
            full,
            half,
            att_far_y.at[i],
            att_near_y.at[i],
            att_far_z.at[i],
            att_near_z.at[i],
        )

    backs = [lambda r=r: back(r) for r in range(CHIPS)]
    run(BACKWARD_ORDER, [key_sums(0), key_sums(1), backs, [send_queries]])
    swaps.append(net.copy(grad_sums.at[0, other_rows, :], pairs.at[1, core], net.sibling))
    swaps.append(net.copy(grad_sums.at[0, other_values, :], pairs.at[2, core], net.sibling))
    pairs[1, core] = grad_sums[0, own_rows, :]
    pairs[2, core] = grad_sums[0, own_values, :]
    for made in swaps:
        made.wait_recv()
    net.finish()


def finish_kernel(pairs, layer_ref, residual_ref, layer_out, residual_out, *outs):
    layer_out[...] = layer_ref[...]
    residual_out[...] = residual_ref[...]
    for i, out in enumerate(outs):
        out[:, :128] = pairs[i, 0]
        out[:, 128:] = pairs[i, 1]


def local(
    residual,
    query_states,
    key_states,
    value_states,
    out_weight,
    norm_gain,
    expert_ids,
    gate_weights,
    gate_matrix,
    up_matrix,
    down_matrix,
    grad_out,
):
    inputs = (
        query_states,
        key_states,
        value_states,
        residual,
        norm_gain.reshape(1, D),
        expert_ids.T,
        gate_weights.T,
        grad_out,
        out_weight,
        gate_matrix.transpose(0, 2, 1),
        up_matrix.transpose(0, 2, 1),
        down_matrix,
    )
    v = lambda *shape: pltpu.VMEM(shape, BF16)
    vmem = pl.BlockSpec(memory_space=pltpu.VMEM)
    results = [(ROWS, D), (ROWS, D), (3, 2, 128, HD)]
    layer_out, grad_residual, pairs = pl.pallas_call(
        layer_kernel,
        out_shape=[jax.ShapeDtypeStruct(shape, BF16) for shape in results],
        in_specs=[vmem] * 8 + [pl.BlockSpec(memory_space=pl.ANY)] * 4,
        out_specs=[vmem] * 3,
        scratch_shapes=[
            v(256, D),
            v(CHIP_ROWS, HD),
            v(CHIPS, 512, HD),
            v(CHIPS, CHIP_ROWS, CHIP_ROWS),
            v(CHIP_ROWS, HD),
            pltpu.VMEM((CHIPS, CHIP_ROWS, CHIP_ROWS), F32),
            pltpu.VMEM((CHIP_ROWS, 128), F32),
            pltpu.VMEM((CHIP_ROWS, 128), F32),
            v(2, 128, HD),
            v(128, D),
            v(128, D),
            v(128, CHUNK),
            v(128, CHUNK),
            v(2, CHIP_ROWS, 2 * D),
            v(2, CHIP_ROWS, 2 * D),
            v(2, 2, HIDDEN, D),
            v(2, 2, HIDDEN, D),
            v(2, 2, HIDDEN, D),
            pltpu.VMEM((2, 2, CHIP_ROWS, HIDDEN), F32),
            pltpu.VMEM((2, 2, CHIP_ROWS, HIDDEN), F32),
            v(2, 2, CHIP_ROWS, HIDDEN),
            v(2, 2, CHIP_ROWS, HIDDEN),
            v(2, 2, CHIP_ROWS, HIDDEN),
            v(4, 2, 2, ROWS, CHUNK),
            v(4, 2, 4, ROWS, D),
            v(4, 2, ROWS, CHUNK),
            v(4, 4, ROWS, D),
            v(128, CHUNK),
            v(128, CHUNK),
            v(128, D),
            v(2, 128, HD),
            v(CHIP_ROWS, HD),
            v(CHIPS, 512, HD),
            pltpu.VMEM((CHIP_ROWS, HD), F32),
            v(128, HD),
            v(2, 2, 2, 128, HD),
            v(2, 2, 4, 256, HD),
            v(2, 2, 128, HD),
            v(2, 4, 256, HD),
            pltpu.SemaphoreType.DMA((4,)),
            pltpu.SemaphoreType.DMA((COPIES,)),
            pltpu.SemaphoreType.DMA((COPIES,)),
        ],
        compiler_params=pltpu.CompilerParams(
            collective_id=0, has_side_effects=True, vmem_limit_bytes=VMEM_LIMIT
        ),
        cost_estimate=pl.CostEstimate(
            flops=8 * 10**9, bytes_accessed=1 << 24, transcendentals=1 << 21
        ),
    )(*inputs)
    shapes = [(ROWS, D)] * 2 + [(128, 2 * HD)] * 3
    return pl.pallas_call(
        finish_kernel,
        out_shape=[jax.ShapeDtypeStruct(shape, BF16) for shape in shapes],
    )(pairs, layer_out, grad_residual)


def solution(mesh):
    in_specs = (
        P(("ctx", "exp"), None),
        P("ctx", "exp"),
        P("ctx", "exp"),
        P("ctx", "exp"),
        P("exp", None),
        P(),
        P(("ctx", "exp"), None),
        P(("ctx", "exp"), None),
        P("exp", None, "ctx"),
        P("exp", None, "ctx"),
        P("exp", "ctx", None),
        P(("ctx", "exp"), None),
    )
    out_specs = (
        P(("ctx", "exp"), None),
        P(("ctx", "exp"), None),
        P("ctx", "exp"),
        P("ctx", "exp"),
        P("ctx", "exp"),
    )
    return jax.shard_map(local, mesh=mesh, in_specs=in_specs, out_specs=out_specs, check_vma=False)
```

```python
import math

import jax
import jax.numpy as jnp
from jax import lax
from jax.experimental import pallas as pl
from jax.experimental.pallas import tpu as pltpu
from jax.sharding import PartitionSpec as P

MESH = pl.DeviceIdType.MESH
F32 = jnp.float32
BF16 = jnp.bfloat16
HD = 128
D = 2048
ROWS = 16
CHIPS = 16
N_EXP = 8
CHIP_ROWS = 256
HIDDEN = 200
CHUNK = 1024
QUARTER = 512
EPSILON = 1e-05
MASKED = -1e30
SCALE = 1.0 / math.sqrt(HD)
VMEM_LIMIT = 58 * 1024 * 1024
COPIES = 270

ORDER = (
    0, 1, 16, 258, 17, 2, 257, 18, 3, 4, 20, 19, 5, 21, 259, 80, 6, 256, 8, 7, 22, 24, 48, 264, 9,
    12, 23, 25, 81, 11, 10, 240, 243, 242, 27, 241, 26, 28, 260, 49, 52, 261, 83, 82, 51, 84, 262,
    55, 54, 86, 85, 263, 32, 33, 64, 87, 65, 57, 50, 34, 66, 35, 36, 56, 37, 68, 38, 67, 89, 53, 69,
    40, 58, 91, 41, 39, 70, 43, 44, 42, 97, 96, 59, 60, 99, 73, 98, 105, 106, 92, 88, 90, 104, 107,
    145, 144, 146, 75, 76, 72, 71, 74, 113, 112, 114, 115, 121, 148, 120, 122, 123, 176, 177, 100,
    147, 102, 103, 119, 101, 118, 151, 129, 180, 179, 178, 128, 116, 149, 181, 183, 132, 153, 155,
    152, 154, 185, 182, 184, 186, 187, 150, 135, 130, 117, 161, 156, 157, 131, 188, 189, 265, 160,
    164, 167, 266, 137, 139, 162, 133, 163, 136, 138, 168, 165, 169, 171, 134, 166, 170, 267, 268,
    202, 225, 203, 201, 224, 208, 209, 207, 200, 206, 198, 228, 194, 204, 199, 212, 227, 231, 205,
    197, 226, 215, 211, 172, 140, 141, 173, 210, 269, 196, 213, 195, 233, 229, 193, 232, 234, 235,
    216, 218, 217, 219, 214, 192, 271, 270, 230, 220, 236, 237, 221,
)
NT = (((1,), (1,)), ((), ()))
TN = (((0,), (0,)), ((), ()))


def rel(dy, dz):
    return dy * 4 + dz


class Net:
    def __init__(self, send, recv):
        self.send, self.recv, self.count, self.started = send, recv, 0, []
        ctx = lax.axis_index("ctx")
        self.exp = lax.axis_index("exp")
        self.core = lax.rem(ctx, 2)
        chip = ctx // 2
        self.y, self.z = chip // 4, lax.rem(chip, 4)
        at = lambda y, z, c: {"ctx": (lax.rem(y, 4) * 4 + lax.rem(z, 4)) * 2 + c}
        self.yp = at(self.y + 1, self.z, self.core)
        self.ym = at(self.y + 3, self.z, self.core)
        self.zp = at(self.y, self.z + 1, self.core)
        self.zm = at(self.y, self.z + 3, self.core)
        self.sibling = at(self.y, self.z, 1 - self.core)
        self.peers = [lax.rem(self.exp + d, N_EXP) for d in range(1, N_EXP)]

    def copy(self, src, dst, device):
        i = self.count
        self.count += 1
        made = pltpu.make_async_remote_copy(
            src_ref=src,
            dst_ref=dst,
            send_sem=self.send.at[i],
            recv_sem=self.recv.at[i],
            device_id=device,
            device_id_type=MESH,
        )
        made.start()
        self.started.append(made)
        return made

    def finish(self):
        for made in self.started:
            made.wait_send()

    def barrier(self, devices):
        sem = pltpu.get_barrier_semaphore()
        for device in devices:
            pl.semaphore_signal(sem, inc=1, device_id=device, device_id_type=MESH)
        pl.semaphore_wait(sem, len(devices))

    def ring_devices(self):
        return [self.yp, self.ym, self.zp, self.zm]

    def peer_devices(self):
        return [{"exp": peer} for peer in self.peers]

    def push(self, src_of, dst):
        return [self.copy(src_of(peer), dst, {"exp": peer}) for peer in self.peers]


def gather_steps(net, full, half, seen=lambda r: None):
    state = {}

    def send_z():
        state["z3"] = net.copy(full(rel(0, 0)), full(rel(0, 3)), net.zp)
        state["z1"] = net.copy(full(rel(0, 0)), full(rel(0, 1)), net.zm)

    def send_y(dz):
        state["y3", dz] = net.copy(full(rel(0, dz)), full(rel(3, dz)), net.yp)
        state["y1", dz] = net.copy(full(rel(0, dz)), full(rel(1, dz)), net.ym)

    def near_z3():
        state["z3"].wait_recv()
        state["h0"] = net.copy(half(rel(0, 3), 0), half(rel(0, 2), 0), net.zp)
        send_y(3)
        seen(rel(0, 3))

    def near_z1():
        state["z1"].wait_recv()
        state["h1"] = net.copy(half(rel(0, 1), 1), half(rel(0, 2), 1), net.zm)
        send_y(1)
        seen(rel(0, 1))

    def far_z():
        state["h0"].wait_recv()
        state["h1"].wait_recv()
        send_y(2)
        seen(rel(0, 2))

    def near_y(dz):
        state["y3", dz].wait_recv()
        state["y1", dz].wait_recv()
        if dz in (0, 2):
            state["g0", dz] = net.copy(half(rel(3, dz), 0), half(rel(2, dz), 0), net.yp)
            state["g1", dz] = net.copy(half(rel(1, dz), 1), half(rel(2, dz), 1), net.ym)
        seen(rel(3, dz))
        seen(rel(1, dz))

    def far_y(dz):
        state["g0", dz].wait_recv()
        state["g1", dz].wait_recv()
        if dz == 0:
            state["f3"] = net.copy(full(rel(2, 0)), full(rel(2, 3)), net.zp)
            state["f1"] = net.copy(full(rel(2, 0)), full(rel(2, 1)), net.zm)
        seen(rel(2, dz))

    def end(dz):
        state["f%d" % dz].wait_recv()
        seen(rel(2, dz))

    return [
        send_z,
        lambda: send_y(0),
        lambda: near_y(0),
        near_z3,
        near_z1,
        lambda: far_y(0),
        far_z,
        lambda: near_y(3),
        lambda: near_y(1),
        lambda: near_y(2),
        lambda: far_y(2),
        lambda: end(3),
        lambda: end(1),
    ]


def reduce_steps(net, full, half, far_y, near_y, far_z, near_z):
    ra, rb, za, zb = far_y.at[0], far_y.at[1], far_z.at[0], far_z.at[1]
    rc, rd = near_y.at[0], near_y.at[1]
    zc, zd, ze, zf = [near_z.at[i] for i in range(4)]
    state = {}

    def add(target, *sources):
        total = target[...].astype(F32)
        for source in sources:
            total = total + source[...].astype(F32)
        target[...] = total.astype(BF16)

    def send_far_z():
        state["e"] = net.copy(full(rel(2, 1)), ze, net.zp)
        state["f"] = net.copy(full(rel(2, 3)), zf, net.zm)

    def send_far_y(dz):
        if dz == 0:
            state["e"].wait_recv()
            state["f"].wait_recv()
            add(full(rel(2, 0)), ze, zf)
        state["a", dz] = net.copy(half(rel(2, dz), 0), ra.at[dz // 2], net.yp)
        state["b", dz] = net.copy(half(rel(2, dz), 1), rb.at[dz // 2], net.ym)

    def send_near(dz):
        if dz in (0, 2):
            state["a", dz].wait_recv()
            state["b", dz].wait_recv()
            add(half(rel(1, dz), 0), ra.at[dz // 2])
            add(half(rel(3, dz), 1), rb.at[dz // 2])
        state["c", dz] = net.copy(full(rel(1, dz)), rc.at[dz], net.yp)
        state["d", dz] = net.copy(full(rel(3, dz)), rd.at[dz], net.ym)

    def collect(dz):
        state["c", dz].wait_recv()
        state["d", dz].wait_recv()
        add(full(rel(0, dz)), rc.at[dz], rd.at[dz])
        if dz == 2:
            state["za"] = net.copy(half(rel(0, 2), 0), za, net.zp)
            state["zb"] = net.copy(half(rel(0, 2), 1), zb, net.zm)

    def send_z1():
        state["za"].wait_recv()
        add(half(rel(0, 1), 0), za)
        state["zc"] = net.copy(full(rel(0, 1)), zc, net.zp)

    def send_z3():
        state["zb"].wait_recv()
        add(half(rel(0, 3), 1), zb)
        state["zd"] = net.copy(full(rel(0, 3)), zd, net.zm)

    def last():
        state["zc"].wait_recv()
        state["zd"].wait_recv()
        add(full(rel(0, 0)), zc, zd)

    return [
        send_far_z,
        lambda: send_far_y(2),
        lambda: send_near(1),
        lambda: send_near(3),
        lambda: send_near(2),
        lambda: send_far_y(0),
        lambda: send_near(0),
        lambda: collect(2),
        lambda: collect(1),
        lambda: collect(3),
        send_z1,
        send_z3,
        lambda: collect(0),
        last,
    ]


def run(order, parts):
    assert sorted(order) == [16 * p + s for p, part in enumerate(parts) for s in range(len(part))]
    for code in order:
        parts[code // 16][code % 16]()


def column(ref, k):
    diagonal = lax.broadcasted_iota(jnp.int32, (ROWS, ROWS), 0) == lax.broadcasted_iota(
        jnp.int32, (ROWS, ROWS), 1
    )
    row = jnp.broadcast_to(ref[k : k + 1, :], (ROWS, ROWS))
    return jnp.sum(jnp.where(diagonal, row, jnp.zeros_like(row)), axis=1, keepdims=True)


def places(ids_ref):
    lanes = lax.broadcasted_iota(jnp.int32, (ROWS, 128), 1)
    ids = [column(ids_ref, k) for k in range(2)]
    chosen = [(lanes == one).astype(F32) for one in ids]
    lower = (
        lax.broadcasted_iota(jnp.int32, (ROWS, ROWS), 1)
        < lax.broadcasted_iota(jnp.int32, (ROWS, ROWS), 0)
    ).astype(BF16)
    earlier = jnp.dot(lower, (chosen[0] + chosen[1]).astype(BF16), preferred_element_type=F32)
    found = []
    for one, hot in zip(ids, chosen):
        rank = jnp.sum(earlier * hot, axis=1, keepdims=True).astype(jnp.int32)
        place = (one >> 1) * 16 + (one & 1) * 2 + rank
        found.append(jnp.where(rank < 2, place, -1000))
    return found


def one_hot(place, quarter):
    lanes = lax.broadcasted_iota(jnp.int32, (ROWS, 128), 1)
    return (lanes == place + 4 * quarter).astype(BF16)


def packing(quarter, transposed):
    shape, slot_dim = ((128, 32), 1) if transposed else ((32, 128), 0)
    slot = lax.broadcasted_iota(jnp.int32, shape, slot_dim)
    packed = lax.broadcasted_iota(jnp.int32, shape, 1 - slot_dim)
    want = ((slot & 15) >> 1) * 16 + quarter * 4 + (slot >> 4) * 2 + (slot & 1)
    return (packed == want).astype(BF16)


def layer_kernel(
    q_ref,
    k_ref,
    v_ref,
    residual_ref,
    gain_ref,
    ids_ref,
    gw_ref,
    go_ref,
    ow_hbm,
    wg_hbm,
    wu_hbm,
    wd_hbm,
    layer_out,
    residual_out,
    pairs,
    ow_ref,
    queries,
    kv,
    softmax,
    attended_rows,
    scores,
    row_top,
    row_sum,
    att_pair,
    partial,
    pieces,
    packed,
    arrived,
    slots,
    sums,
    gates,
    ups,
    downs,
    gate_part,
    up_part,
    actives,
    grad_gates,
    grad_ups,
    far_y,
    near_y,
    far_z,
    near_z,
    returned,
    hidden_rows,
    delta_rows,
    slab,
    grads,
    grad_heads,
    grad_sums,
    dq_rows,
    dq_other,
    att_far_y,
    att_near_y,
    att_far_z,
    att_near_z,
    load_sem,
    send,
    recv,
):
    net = Net(send, recv)
    core, me = net.core, net.exp
    own_rows = pl.ds(pl.multiple_of(core * 128, 128), 128)
    other_rows = pl.ds(pl.multiple_of((1 - core) * 128, 128), 128)
    own_values = pl.ds(pl.multiple_of(256 + core * 128, 128), 128)
    other_values = pl.ds(pl.multiple_of(256 + (1 - core) * 128, 128), 128)

    def piece(ref, peer):
        return ref.at[pl.ds(pl.multiple_of(peer * ROWS, ROWS), ROWS), :]

    def mine(ref):
        return jnp.where(core == 0, ref[:, :128], ref[:, 128:])

    weights = ((wg_hbm, gates), (wu_hbm, ups), (wd_hbm, downs))
    loads = [pltpu.make_async_copy(ow_hbm, ow_ref, load_sem.at[0])]
    for i, (source, target) in enumerate(weights):
        loads.append(pltpu.make_async_copy(source, target.at[0], load_sem.at[i + 1]))
    for made in loads:
        made.start()
    net.barrier(net.ring_devices() + [net.sibling] + net.peer_devices())

    exchange = [
        net.copy(k_ref.at[:, other_rows], kv.at[0, own_rows, :], net.sibling),
        net.copy(q_ref.at[:, other_rows], queries.at[own_rows, :], net.sibling),
        net.copy(v_ref.at[:, other_rows], kv.at[0, own_values, :], net.sibling),
    ]
    kv[0, own_rows, :] = mine(k_ref)
    kv[0, own_values, :] = mine(v_ref)
    queries[own_rows, :] = mine(q_ref)

    chip = net.y * 4 + net.z

    def score_block(r):
        dy, dz = r // 4, r % 4
        other = lax.rem(net.y + dy, 4) * 4 + lax.rem(net.z + dz, 4)
        s = lax.dot_general(queries[...], kv[r, :256, :], NT, preferred_element_type=F32) * SCALE
        row = lax.broadcasted_iota(jnp.int32, (CHIP_ROWS, CHIP_ROWS), 0) + chip * CHIP_ROWS
        place = lax.broadcasted_iota(jnp.int32, (CHIP_ROWS, CHIP_ROWS), 1) + other * CHIP_ROWS
        s = jnp.where(place <= row, s, MASKED)
        scores[r] = s
        row_top[...] = jnp.maximum(row_top[...], jnp.maximum(s[:, :128], s[:, 128:]))

    row_top[...] = jnp.full((CHIP_ROWS, 128), MASKED, F32)
    row_sum[...] = jnp.zeros((CHIP_ROWS, 128), F32)

    def raise_blocks(quarter):
        m = jnp.max(row_top[...], axis=1, keepdims=True)

        def one(r, total):
            e = jnp.exp(scores[r] - m)
            scores[r] = e
            return total + (e[:, :128] + e[:, 128:])

        row_sum[...] = lax.fori_loop(4 * quarter, 4 * quarter + 4, one, row_sum[...])

    def pair(start, seen):
        full = lambda r: kv.at[r, pl.ds(start, 256), :]
        half = lambda r, h: kv.at[r, pl.ds(start + h * 128, 128), :]
        return gather_steps(net, full, half, seen)

    keep = {}

    def send_weights():
        keep["weights"] = [net.copy(hbm, at.at[1], net.sibling) for hbm, at in weights]

    def wait_for(name):
        for made in keep.pop(name):
            made.wait_recv()

    found = places(ids_ref)
    weight = [column(gw_ref, k) for k in range(2)]

    def exchange_slots(name, source, target):
        keep[name] = net.push(lambda peer: piece(source, peer), piece(target, me))
        piece(target, me)[...] = piece(source, me)[...]

    def pack(part, rows_of):
        for quarter in range(4):
            columns = slice(quarter * QUARTER, (quarter + 1) * QUARTER)
            spread = rows_of(quarter, columns)
            total = spread if quarter == 0 else total + spread
        packed[part] = total.astype(BF16)

    def dispatch_weighted():
        grad_out = go_ref[...].astype(F32)
        weighted = [(weight[k] * grad_out).astype(BF16) for k in range(2)]

        def rows_of(quarter, columns):
            return sum(
                lax.dot_general(
                    one_hot(found[k], quarter),
                    weighted[k][:, columns],
                    TN,
                    preferred_element_type=F32,
                )
                for k in range(2)
            )

        pack(1, rows_of)
        exchange_slots("arrived1", packed.at[1], arrived.at[1])

    def unpack(part):
        wait_for("arrived%d" % part)
        for quarter in range(4):
            rows = jnp.dot(packing(quarter, False), arrived[part], preferred_element_type=F32)
            rows = rows.astype(BF16)
            low = part * D + quarter * QUARTER
            for e in range(2):
                slots[e, 0:ROWS, low : low + QUARTER] = rows[e * ROWS : (e + 1) * ROWS]

    def attend():
        inverse = 1.0 / jnp.sum(row_sum[...], axis=1, keepdims=True)

        def one(r, acc):
            low = (scores[r] * inverse).astype(BF16)
            softmax[r] = low
            return acc + jnp.dot(low, kv[r, 256:, :], preferred_element_type=F32)

        attended = lax.fori_loop(0, CHIPS, one, jnp.zeros((CHIP_ROWS, HD), F32))
        attended_rows[...] = attended.astype(BF16)
        keep["attended"] = [
            net.copy(attended_rows.at[other_rows, :], att_pair.at[core], net.sibling)
        ]
        att_pair[core] = attended_rows[own_rows, :]

    def project():
        for made in loads:
            made.wait()
        wait_for("attended")
        for n in range(4):
            columns = pl.ds(n * 512, 512)
            partial[:, columns] = (
                jnp.dot(att_pair[0], ow_ref[:128, columns], preferred_element_type=F32)
                + jnp.dot(att_pair[1], ow_ref[128:, columns], preferred_element_type=F32)
            ).astype(BF16)
        exchange_slots("projected", partial, pieces)

    def inverse_norm():
        wide = hidden_rows[...]
        return lax.rsqrt(jnp.mean(wide * wide, axis=1, keepdims=True) + EPSILON)

    def norm():
        wait_for("projected")
        projected = pieces[0:ROWS, :].astype(F32)
        for j in range(1, N_EXP):
            projected = projected + pieces[j * ROWS : (j + 1) * ROWS, :].astype(F32)
        hidden = (residual_ref[...].astype(F32) + projected).astype(BF16)
        hidden_rows[...] = hidden.astype(F32)
        normed = (hidden_rows[...] * inverse_norm() * gain_ref[...]).astype(BF16)

        def rows_of(quarter, columns):
            hot = one_hot(found[0], quarter) + one_hot(found[1], quarter)
            return lax.dot_general(hot, normed[:, columns], TN, preferred_element_type=F32)

        pack(0, rows_of)
        exchange_slots("arrived0", packed.at[0], arrived.at[0])

    def block(ref, e, part):
        full = lambda r: ref.at[e, pl.ds(r * ROWS, ROWS), pl.ds(part * D, D)]
        half = lambda r, h: ref.at[
            e, pl.ds(r * ROWS, ROWS), pl.ds(part * D + h * CHUNK, CHUNK)
        ]
        return full, half

    parts = [(e, part) for e in range(2) for part in range(2)]
    gathers = [gather_steps(net, *block(slots, e, part)) for e, part in parts]
    reduces = []
    for i, (e, part) in enumerate(parts):
        buffers = [ref.at[i] for ref in (far_y, near_y, far_z, near_z)]
        reduces.append(reduce_steps(net, *block(sums, e, part), *buffers))

    def compute_steps(e):
        def enter(half):
            inputs = slots[e, :, :D]
            gate = lax.dot_general(inputs, gates[half, e], NT, preferred_element_type=F32)
            up = lax.dot_general(inputs, ups[half, e], NT, preferred_element_type=F32)
            gate_part[e, half] = gate
            up_part[e, half] = up
            actives[e, half] = (gate * jax.nn.sigmoid(gate) * up).astype(BF16)

        def enter_grad(half):
            grad = lax.dot_general(
                slots[e, :, D:], downs[half, e], NT, preferred_element_type=F32
            )
            gate, up = gate_part[e, half], up_part[e, half]
            s = jax.nn.sigmoid(gate)
            grad_gates[e, half] = (grad * up * s * (1.0 + gate * (1.0 - s))).astype(BF16)
            grad_ups[e, half] = (grad * gate * s).astype(BF16)

        def leave(n, start, terms):
            columns = pl.ds(n * 512, 512)
            total = jnp.zeros((CHIP_ROWS, 512), F32)
            for half in range(2):
                for rows, matrix in terms:
                    total = total + jnp.dot(
                        rows[e, half], matrix[half, e, :, columns], preferred_element_type=F32
                    )
            sums[e, :, pl.ds(start + n * 512, 512)] = total.astype(BF16)

        out_terms = [(actives, downs)]
        grad_terms = [(grad_gates, gates), (grad_ups, ups)]
        steps = [lambda half=half: enter(half) for half in range(2)]
        steps += [lambda half=half: enter_grad(half) for half in range(2)]
        steps += [lambda n=n: leave(n, 0, out_terms) for n in range(4)]
        steps += [lambda n=n: leave(n, D, grad_terms) for n in range(4)]
        return steps

    def pack_sums(part):
        def rows_of(quarter, columns):
            low = part * D + quarter * QUARTER
            both = [sums[e, 0:ROWS, low : low + QUARTER] for e in range(2)]
            return jnp.dot(
                packing(quarter, True),
                jnp.concatenate(both, axis=0),
                preferred_element_type=F32,
            )

        pack(2 + part, rows_of)
        exchange_slots("returned%d" % part, packed.at[2 + part], returned.at[part])

    def pick(k, part):
        rows = [
            jnp.dot(one_hot(found[k], quarter), returned[part], preferred_element_type=F32)
            for quarter in range(4)
        ]
        return jnp.concatenate(rows, axis=1)

    def residual_gradient():
        wait_for("returned1")
        wide, inverse = hidden_rows[...], inverse_norm()
        scaled = gain_ref[...] * (pick(0, 1) + pick(1, 1))
        cube = inverse * inverse * inverse
        grad_hidden = go_ref[...].astype(F32) + (
            inverse * scaled - wide * cube * jnp.mean(wide * scaled, axis=1, keepdims=True)
        )
        residual_out[...] = grad_hidden.astype(BF16)
        keep["slab"] = net.push(lambda peer: residual_out, piece(slab, me))
        piece(slab, me)[...] = residual_out[...]

    def layer_output():
        wait_for("returned0")
        mixture = weight[0] * pick(0, 0) + weight[1] * pick(1, 0)
        layer_out[...] = (hidden_rows[...] + mixture).astype(BF16)

    def attended_gradient():
        wait_for("slab")
        for head in range(2):
            grads[head] = lax.dot_general(
                slab[...],
                ow_ref[head * 128 : head * 128 + 128, :],
                NT,
                preferred_element_type=F32,
            ).astype(BF16)
        keep["grads"] = [net.copy(grads.at[1 - core], grad_heads.at[own_rows, :], net.sibling)]
        grad_heads[own_rows, :] = grads[core]

    def row_delta():
        wait_for("grads")
        delta_rows[...] = jnp.sum(
            grad_heads[...].astype(F32) * attended_rows[...].astype(F32), axis=1, keepdims=True
        )
        dq_rows[...] = jnp.zeros((CHIP_ROWS, HD), F32)

    def back(r):
        low, grad_head = softmax[r], grad_heads[...]
        grad_prob = lax.dot_general(grad_head, kv[r, 256:, :], NT, preferred_element_type=F32)
        grad_score = (low.astype(F32) * (grad_prob - delta_rows[...])).astype(BF16)
        dq_rows[...] += jnp.dot(grad_score, kv[r, :256, :], preferred_element_type=F32)
        grad_sums[r, :256, :] = (
            lax.dot_general(grad_score, queries[...], TN, preferred_element_type=F32) * SCALE
        ).astype(BF16)
        grad_sums[r, 256:, :] = lax.dot_general(
            low, grad_head, TN, preferred_element_type=F32
        ).astype(BF16)

    def send_queries():
        dq_other[...] = (dq_rows[other_rows, :] * SCALE).astype(BF16)
        keep["queries"] = [net.copy(dq_other, pairs.at[0, core], net.sibling)]
        pairs[0, core] = (dq_rows[own_rows, :] * SCALE).astype(BF16)

    def key_sums(i):
        full = lambda r: grad_sums.at[r, pl.ds(i * 256, 256), :]
        half = lambda r, h: grad_sums.at[r, pl.ds(i * 256 + h * 128, 128), :]
        buffers = [ref.at[i] for ref in (att_far_y, att_near_y, att_far_z, att_near_z)]
        return reduce_steps(net, full, half, *buffers)

    for made in exchange:
        made.wait_recv()
    run(
        ORDER,
        [pair(0, score_block), pair(256, lambda r: None)]
        + gathers
        + [compute_steps(e) for e in range(2)]
        + reduces
        + [[lambda r=r: back(r) for r in range(CHIPS)], key_sums(0), key_sums(1)]
        + [[lambda i=i: raise_blocks(i) for i in range(4)]]
        + [
            [
                lambda: score_block(0),
                send_weights,
                dispatch_weighted,
                lambda: unpack(1),
                attend,
                project,
                norm,
                lambda: unpack(0),
                lambda: wait_for("weights"),
                lambda: pack_sums(1),
                residual_gradient,
                attended_gradient,
                row_delta,
                lambda: pack_sums(0),
                layer_output,
                send_queries,
            ]
        ],
    )
    swaps = [
        net.copy(grad_sums.at[0, other_rows, :], pairs.at[1, core], net.sibling),
        net.copy(grad_sums.at[0, other_values, :], pairs.at[2, core], net.sibling),
    ]
    pairs[1, core] = grad_sums[0, own_rows, :]
    pairs[2, core] = grad_sums[0, own_values, :]
    for made in swaps:
        made.wait_recv()
    wait_for("queries")
    net.finish()


def finish_kernel(pairs, layer_ref, residual_ref, layer_out, residual_out, *outs):
    layer_out[...] = layer_ref[...]
    residual_out[...] = residual_ref[...]
    for i, out in enumerate(outs):
        out[:, :128] = pairs[i, 0]
        out[:, 128:] = pairs[i, 1]


def local(
    residual,
    query_states,
    key_states,
    value_states,
    out_weight,
    norm_gain,
    expert_ids,
    gate_weights,
    gate_matrix,
    up_matrix,
    down_matrix,
    grad_out,
):
    inputs = (
        query_states,
        key_states,
        value_states,
        residual,
        norm_gain.reshape(1, D),
        expert_ids.T,
        gate_weights.T,
        grad_out,
        out_weight,
        gate_matrix.transpose(0, 2, 1),
        up_matrix.transpose(0, 2, 1),
        down_matrix,
    )
    v = lambda *shape: pltpu.VMEM(shape, BF16)
    vmem = pl.BlockSpec(memory_space=pltpu.VMEM)
    results = [(ROWS, D), (ROWS, D), (3, 2, 128, HD)]
    layer_out, grad_residual, pairs = pl.pallas_call(
        layer_kernel,
        out_shape=[jax.ShapeDtypeStruct(shape, BF16) for shape in results],
        in_specs=[vmem] * 8 + [pl.BlockSpec(memory_space=pl.ANY)] * 4,
        out_specs=[vmem] * 3,
        scratch_shapes=[
            v(256, D),
            v(CHIP_ROWS, HD),
            v(CHIPS, 512, HD),
            v(CHIPS, CHIP_ROWS, CHIP_ROWS),
            v(CHIP_ROWS, HD),
            pltpu.VMEM((CHIPS, CHIP_ROWS, CHIP_ROWS), F32),
            pltpu.VMEM((CHIP_ROWS, 128), F32),
            pltpu.VMEM((CHIP_ROWS, 128), F32),
            v(2, 128, HD),
            v(128, D),
            v(128, D),
            v(4, 128, QUARTER),
            v(2, 128, QUARTER),
            v(2, CHIP_ROWS, 2 * D),
            v(2, CHIP_ROWS, 2 * D),
            v(2, 2, HIDDEN, D),
            v(2, 2, HIDDEN, D),
            v(2, 2, HIDDEN, D),
            pltpu.VMEM((2, 2, CHIP_ROWS, HIDDEN), F32),
            pltpu.VMEM((2, 2, CHIP_ROWS, HIDDEN), F32),
            v(2, 2, CHIP_ROWS, HIDDEN),
            v(2, 2, CHIP_ROWS, HIDDEN),
            v(2, 2, CHIP_ROWS, HIDDEN),
            v(4, 2, 2, ROWS, CHUNK),
            v(4, 2, 4, ROWS, D),
            v(4, 2, ROWS, CHUNK),
            v(4, 4, ROWS, D),
            v(2, 128, QUARTER),
            pltpu.VMEM((ROWS, D), F32),
            pltpu.VMEM((CHIP_ROWS, 1), F32),
            v(128, D),
            v(2, 128, HD),
            v(CHIP_ROWS, HD),
            v(CHIPS, 512, HD),
            pltpu.VMEM((CHIP_ROWS, HD), F32),
            v(128, HD),
            v(2, 2, 2, 128, HD),
            v(2, 2, 4, 256, HD),
            v(2, 2, 128, HD),
            v(2, 4, 256, HD),
            pltpu.SemaphoreType.DMA((4,)),
            pltpu.SemaphoreType.DMA((COPIES,)),
            pltpu.SemaphoreType.DMA((COPIES,)),
        ],
        compiler_params=pltpu.CompilerParams(
            collective_id=0, has_side_effects=True, vmem_limit_bytes=VMEM_LIMIT
        ),
        cost_estimate=pl.CostEstimate(
            flops=8 * 10**9, bytes_accessed=1 << 24, transcendentals=1 << 21
        ),
    )(*inputs)
    shapes = [(ROWS, D)] * 2 + [(128, 2 * HD)] * 3
    return pl.pallas_call(
        finish_kernel,
        out_shape=[jax.ShapeDtypeStruct(shape, BF16) for shape in shapes],
    )(pairs, layer_out, grad_residual)


def solution(mesh):
    in_specs = (
        P(("ctx", "exp"), None),
        P("ctx", "exp"),
        P("ctx", "exp"),
        P("ctx", "exp"),
        P("exp", None),
        P(),
        P(("ctx", "exp"), None),
        P(("ctx", "exp"), None),
        P("exp", None, "ctx"),
        P("exp", None, "ctx"),
        P("exp", "ctx", None),
        P(("ctx", "exp"), None),
    )
    out_specs = (
        P(("ctx", "exp"), None),
        P(("ctx", "exp"), None),
        P("ctx", "exp"),
        P("ctx", "exp"),
        P("ctx", "exp"),
    )
    return jax.shard_map(local, mesh=mesh, in_specs=in_specs, out_specs=out_specs, check_vma=False)
```

```python
import math

import jax
import jax.numpy as jnp
from jax import lax
from jax.experimental import pallas as pl
from jax.experimental.pallas import tpu as pltpu
from jax.sharding import PartitionSpec as P

MESH = pl.DeviceIdType.MESH
F32 = jnp.float32
BF16 = jnp.bfloat16
HD = 128
D = 2048
ROWS = 16
CHIPS = 16
N_EXP = 8
CHIP_ROWS = 256
HIDDEN = 200
CHUNK = 1024
QUARTER = 512
EPSILON = 1e-05
MASKED = -1e30
SCALE = 1.0 / math.sqrt(HD)
VMEM_LIMIT = 58 * 1024 * 1024
COPIES = 270

ORDER = (
    0, 1, 17, 16, 258, 2, 18, 3, 4, 19, 20, 5, 21, 6, 256, 22, 259, 23, 8, 7, 9, 12, 48, 11, 24, 25,
    80, 27, 28, 10, 243, 240, 241, 242, 26, 260, 81, 261, 49, 51, 82, 84, 52, 83, 262, 85, 54, 50,
    86, 257, 263, 64, 65, 33, 32, 89, 66, 57, 34, 67, 68, 264, 69, 35, 70, 36, 92, 72, 90, 37, 87,
    71, 56, 91, 73, 39, 53, 88, 38, 75, 55, 76, 58, 40, 74, 113, 112, 114, 41, 115, 121, 120, 123,
    122, 177, 59, 60, 179, 176, 43, 44, 42, 97, 96, 99, 98, 107, 180, 105, 104, 106, 145, 144, 116,
    119, 146, 183, 148, 117, 178, 118, 160, 181, 101, 147, 100, 102, 103, 151, 149, 129, 130, 184,
    185, 187, 152, 186, 182, 153, 161, 154, 155, 150, 128, 132, 188, 164, 156, 189, 131, 157, 265,
    133, 162, 167, 165, 135, 266, 137, 163, 169, 136, 138, 168, 134, 166, 139, 171, 170, 267, 268,
    202, 209, 201, 225, 203, 224, 206, 208, 198, 140, 212, 205, 199, 228, 207, 204, 211, 197, 210,
    226, 172, 173, 194, 215, 195, 193, 141, 231, 269, 227, 200, 229, 213, 192, 216, 217, 218, 219,
    196, 232, 271, 234, 233, 235, 230, 270, 214, 220, 221, 236, 237,
)
NT = (((1,), (1,)), ((), ()))
TN = (((0,), (0,)), ((), ()))


def rel(dy, dz):
    return dy * 4 + dz


class Net:
    def __init__(self, send, recv):
        self.send, self.recv, self.count, self.started = send, recv, 0, []
        ctx = lax.axis_index("ctx")
        self.exp = lax.axis_index("exp")
        self.core = lax.rem(ctx, 2)
        chip = ctx // 2
        self.y, self.z = chip // 4, lax.rem(chip, 4)
        at = lambda y, z, c: {"ctx": (lax.rem(y, 4) * 4 + lax.rem(z, 4)) * 2 + c}
        self.yp = at(self.y + 1, self.z, self.core)
        self.ym = at(self.y + 3, self.z, self.core)
        self.zp = at(self.y, self.z + 1, self.core)
        self.zm = at(self.y, self.z + 3, self.core)
        self.sibling = at(self.y, self.z, 1 - self.core)
        self.peers = [lax.rem(self.exp + d, N_EXP) for d in range(1, N_EXP)]

    def copy(self, src, dst, device):
        i = self.count
        self.count += 1
        made = pltpu.make_async_remote_copy(
            src_ref=src,
            dst_ref=dst,
            send_sem=self.send.at[i],
            recv_sem=self.recv.at[i],
            device_id=device,
            device_id_type=MESH,
        )
        made.start()
        self.started.append(made)
        return made

    def wait(self, made):
        for _ in range(3):
            if len(self.started) > 48:
                self.started.pop(0).wait_send()
        made.wait_recv()

    def finish(self):
        for made in self.started:
            made.wait_send()

    def barrier(self, devices):
        sem = pltpu.get_barrier_semaphore()
        for device in devices:
            pl.semaphore_signal(sem, inc=1, device_id=device, device_id_type=MESH)
        pl.semaphore_wait(sem, len(devices))

    def ring_devices(self):
        return [self.yp, self.ym, self.zp, self.zm]

    def peer_devices(self):
        return [{"exp": peer} for peer in self.peers]

    def push(self, src_of, dst):
        return [self.copy(src_of(peer), dst, {"exp": peer}) for peer in self.peers]


def gather_steps(net, full, half, seen=lambda r: None):
    state = {}

    def send_z():
        state["z3"] = net.copy(full(rel(0, 0)), full(rel(0, 3)), net.zp)
        state["z1"] = net.copy(full(rel(0, 0)), full(rel(0, 1)), net.zm)

    def send_y(dz):
        state["y3", dz] = net.copy(full(rel(0, dz)), full(rel(3, dz)), net.yp)
        state["y1", dz] = net.copy(full(rel(0, dz)), full(rel(1, dz)), net.ym)

    def near_z3():
        net.wait(state["z3"])
        state["h0"] = net.copy(half(rel(0, 3), 0), half(rel(0, 2), 0), net.zp)
        send_y(3)
        seen(rel(0, 3))

    def near_z1():
        net.wait(state["z1"])
        state["h1"] = net.copy(half(rel(0, 1), 1), half(rel(0, 2), 1), net.zm)
        send_y(1)
        seen(rel(0, 1))

    def far_z():
        net.wait(state["h0"])
        net.wait(state["h1"])
        send_y(2)
        seen(rel(0, 2))

    def near_y(dz):
        net.wait(state["y3", dz])
        net.wait(state["y1", dz])
        if dz in (0, 2):
            state["g0", dz] = net.copy(half(rel(3, dz), 0), half(rel(2, dz), 0), net.yp)
            state["g1", dz] = net.copy(half(rel(1, dz), 1), half(rel(2, dz), 1), net.ym)
        seen(rel(3, dz))
        seen(rel(1, dz))

    def far_y(dz):
        net.wait(state["g0", dz])
        net.wait(state["g1", dz])
        if dz == 0:
            state["f3"] = net.copy(full(rel(2, 0)), full(rel(2, 3)), net.zp)
            state["f1"] = net.copy(full(rel(2, 0)), full(rel(2, 1)), net.zm)
        seen(rel(2, dz))

    def end(dz):
        net.wait(state["f%d" % dz])
        seen(rel(2, dz))

    return [
        send_z,
        lambda: send_y(0),
        lambda: near_y(0),
        near_z3,
        near_z1,
        lambda: far_y(0),
        far_z,
        lambda: near_y(3),
        lambda: near_y(1),
        lambda: near_y(2),
        lambda: far_y(2),
        lambda: end(3),
        lambda: end(1),
    ]


def reduce_steps(net, full, half, far_y, near_y, far_z, near_z):
    ra, rb, za, zb = far_y.at[0], far_y.at[1], far_z.at[0], far_z.at[1]
    rc, rd = near_y.at[0], near_y.at[1]
    zc, zd, ze, zf = [near_z.at[i] for i in range(4)]
    state = {}

    def add(target, *sources):
        total = target[...].astype(F32)
        for source in sources:
            total = total + source[...].astype(F32)
        target[...] = total.astype(BF16)

    def send_far_z():
        state["e"] = net.copy(full(rel(2, 1)), ze, net.zp)
        state["f"] = net.copy(full(rel(2, 3)), zf, net.zm)

    def send_far_y(dz):
        if dz == 0:
            net.wait(state["e"])
            net.wait(state["f"])
            add(full(rel(2, 0)), ze, zf)
        state["a", dz] = net.copy(half(rel(2, dz), 0), ra.at[dz // 2], net.yp)
        state["b", dz] = net.copy(half(rel(2, dz), 1), rb.at[dz // 2], net.ym)

    def send_near(dz):
        if dz in (0, 2):
            net.wait(state["a", dz])
            net.wait(state["b", dz])
            add(half(rel(1, dz), 0), ra.at[dz // 2])
            add(half(rel(3, dz), 1), rb.at[dz // 2])
        state["c", dz] = net.copy(full(rel(1, dz)), rc.at[dz], net.yp)
        state["d", dz] = net.copy(full(rel(3, dz)), rd.at[dz], net.ym)

    def collect(dz):
        net.wait(state["c", dz])
        net.wait(state["d", dz])
        add(full(rel(0, dz)), rc.at[dz], rd.at[dz])
        if dz == 2:
            state["za"] = net.copy(half(rel(0, 2), 0), za, net.zp)
            state["zb"] = net.copy(half(rel(0, 2), 1), zb, net.zm)

    def send_z1():
        net.wait(state["za"])
        add(half(rel(0, 1), 0), za)
        state["zc"] = net.copy(full(rel(0, 1)), zc, net.zp)

    def send_z3():
        net.wait(state["zb"])
        add(half(rel(0, 3), 1), zb)
        state["zd"] = net.copy(full(rel(0, 3)), zd, net.zm)

    def last():
        net.wait(state["zc"])
        net.wait(state["zd"])
        add(full(rel(0, 0)), zc, zd)

    return [
        send_far_z,
        lambda: send_far_y(2),
        lambda: send_near(1),
        lambda: send_near(3),
        lambda: send_near(2),
        lambda: send_far_y(0),
        lambda: send_near(0),
        lambda: collect(2),
        lambda: collect(1),
        lambda: collect(3),
        send_z1,
        send_z3,
        lambda: collect(0),
        last,
    ]


def run(order, parts):
    assert sorted(order) == [16 * p + s for p, part in enumerate(parts) for s in range(len(part))]
    for code in order:
        parts[code // 16][code % 16]()


def column(ref, k):
    diagonal = lax.broadcasted_iota(jnp.int32, (ROWS, ROWS), 0) == lax.broadcasted_iota(
        jnp.int32, (ROWS, ROWS), 1
    )
    row = jnp.broadcast_to(ref[k : k + 1, :], (ROWS, ROWS))
    return jnp.sum(jnp.where(diagonal, row, jnp.zeros_like(row)), axis=1, keepdims=True)


def places(ids_ref):
    lanes = lax.broadcasted_iota(jnp.int32, (ROWS, 128), 1)
    ids = [column(ids_ref, k) for k in range(2)]
    chosen = [(lanes == one).astype(F32) for one in ids]
    lower = (
        lax.broadcasted_iota(jnp.int32, (ROWS, ROWS), 1)
        < lax.broadcasted_iota(jnp.int32, (ROWS, ROWS), 0)
    ).astype(BF16)
    earlier = jnp.dot(lower, (chosen[0] + chosen[1]).astype(BF16), preferred_element_type=F32)
    found = []
    for one, hot in zip(ids, chosen):
        rank = jnp.sum(earlier * hot, axis=1, keepdims=True).astype(jnp.int32)
        place = (one >> 1) * 16 + (one & 1) * 2 + rank
        found.append(jnp.where(rank < 2, place, -1000))
    return found


def one_hot(place, quarter):
    lanes = lax.broadcasted_iota(jnp.int32, (ROWS, 128), 1)
    return (lanes == place + 4 * quarter).astype(BF16)


def packing(quarter, transposed):
    shape, slot_dim = ((128, 32), 1) if transposed else ((32, 128), 0)
    slot = lax.broadcasted_iota(jnp.int32, shape, slot_dim)
    packed = lax.broadcasted_iota(jnp.int32, shape, 1 - slot_dim)
    want = ((slot & 15) >> 1) * 16 + quarter * 4 + (slot >> 4) * 2 + (slot & 1)
    return (packed == want).astype(BF16)


def layer_kernel(
    q_ref,
    k_ref,
    v_ref,
    residual_ref,
    gain_ref,
    ids_ref,
    gw_ref,
    go_ref,
    ow_hbm,
    wg_hbm,
    wu_hbm,
    wd_hbm,
    layer_out,
    residual_out,
    pairs,
    ow_ref,
    queries,
    kv,
    softmax,
    attended_rows,
    scores,
    row_top,
    row_sum,
    att_pair,
    partial,
    pieces,
    packed,
    arrived,
    slots,
    sums,
    gates,
    ups,
    downs,
    gate_part,
    up_part,
    actives,
    grad_gates,
    grad_ups,
    far_y,
    near_y,
    far_z,
    near_z,
    returned,
    hidden_rows,
    delta_rows,
    slab,
    grads,
    grad_heads,
    grad_sums,
    dq_rows,
    dq_other,
    att_far_y,
    att_near_y,
    att_far_z,
    att_near_z,
    load_sem,
    send,
    recv,
):
    net = Net(send, recv)
    core, me = net.core, net.exp
    own_rows = pl.ds(pl.multiple_of(core * 128, 128), 128)
    other_rows = pl.ds(pl.multiple_of((1 - core) * 128, 128), 128)
    own_values = pl.ds(pl.multiple_of(256 + core * 128, 128), 128)
    other_values = pl.ds(pl.multiple_of(256 + (1 - core) * 128, 128), 128)

    def piece(ref, peer):
        return ref.at[pl.ds(pl.multiple_of(peer * ROWS, ROWS), ROWS), :]

    def mine(ref):
        return jnp.where(core == 0, ref[:, :128], ref[:, 128:])

    weights = ((wg_hbm, gates), (wu_hbm, ups), (wd_hbm, downs))
    loads = [pltpu.make_async_copy(ow_hbm, ow_ref, load_sem.at[0])]
    for i, (source, target) in enumerate(weights):
        loads.append(pltpu.make_async_copy(source, target.at[0], load_sem.at[i + 1]))
    for made in loads:
        made.start()
    net.barrier(net.ring_devices() + [net.sibling] + net.peer_devices())

    exchange = [
        net.copy(k_ref.at[:, other_rows], kv.at[0, own_rows, :], net.sibling),
        net.copy(q_ref.at[:, other_rows], queries.at[own_rows, :], net.sibling),
        net.copy(v_ref.at[:, other_rows], kv.at[0, own_values, :], net.sibling),
    ]
    kv[0, own_rows, :] = mine(k_ref)
    kv[0, own_values, :] = mine(v_ref)
    queries[own_rows, :] = mine(q_ref)

    chip = net.y * 4 + net.z

    def score_block(r):
        dy, dz = r // 4, r % 4
        other = lax.rem(net.y + dy, 4) * 4 + lax.rem(net.z + dz, 4)
        s = lax.dot_general(queries[...], kv[r, :256, :], NT, preferred_element_type=F32) * SCALE
        row = lax.broadcasted_iota(jnp.int32, (CHIP_ROWS, CHIP_ROWS), 0) + chip * CHIP_ROWS
        place = lax.broadcasted_iota(jnp.int32, (CHIP_ROWS, CHIP_ROWS), 1) + other * CHIP_ROWS
        s = jnp.where(place <= row, s, MASKED)
        scores[r] = s
        row_top[...] = jnp.maximum(row_top[...], jnp.maximum(s[:, :128], s[:, 128:]))

    row_top[...] = jnp.full((CHIP_ROWS, 128), MASKED, F32)
    row_sum[...] = jnp.zeros((CHIP_ROWS, 128), F32)

    def raise_blocks(quarter):
        m = jnp.max(row_top[...], axis=1, keepdims=True)

        def one(r, total):
            e = jnp.exp(scores[r] - m)
            scores[r] = e
            return total + (e[:, :128] + e[:, 128:])

        row_sum[...] = lax.fori_loop(4 * quarter, 4 * quarter + 4, one, row_sum[...])

    def pair(start, seen):
        full = lambda r: kv.at[r, pl.ds(start, 256), :]
        half = lambda r, h: kv.at[r, pl.ds(start + h * 128, 128), :]
        return gather_steps(net, full, half, seen)

    keep = {}

    def send_weights():
        keep["weights"] = [net.copy(hbm, at.at[1], net.sibling) for hbm, at in weights]

    def wait_for(name):
        for made in keep.pop(name):
            net.wait(made)

    found = places(ids_ref)
    weight = [column(gw_ref, k) for k in range(2)]

    def exchange_slots(name, source, target):
        keep[name] = net.push(lambda peer: piece(source, peer), piece(target, me))
        piece(target, me)[...] = piece(source, me)[...]

    def pack(part, rows_of):
        for quarter in range(4):
            columns = slice(quarter * QUARTER, (quarter + 1) * QUARTER)
            spread = rows_of(quarter, columns)
            total = spread if quarter == 0 else total + spread
        packed[part] = total.astype(BF16)

    def dispatch_weighted():
        grad_out = go_ref[...].astype(F32)
        weighted = [(weight[k] * grad_out).astype(BF16) for k in range(2)]

        def rows_of(quarter, columns):
            return sum(
                lax.dot_general(
                    one_hot(found[k], quarter),
                    weighted[k][:, columns],
                    TN,
                    preferred_element_type=F32,
                )
                for k in range(2)
            )

        pack(1, rows_of)
        exchange_slots("arrived1", packed.at[1], arrived.at[1])

    def unpack(part):
        wait_for("arrived%d" % part)
        for quarter in range(4):
            rows = jnp.dot(packing(quarter, False), arrived[part], preferred_element_type=F32)
            rows = rows.astype(BF16)
            low = part * D + quarter * QUARTER
            for e in range(2):
                slots[e, 0:ROWS, low : low + QUARTER] = rows[e * ROWS : (e + 1) * ROWS]

    def attend():
        inverse = 1.0 / jnp.sum(row_sum[...], axis=1, keepdims=True)

        def one(r, acc):
            low = (scores[r] * inverse).astype(BF16)
            softmax[r] = low
            return acc + jnp.dot(low, kv[r, 256:, :], preferred_element_type=F32)

        attended = lax.fori_loop(0, CHIPS, one, jnp.zeros((CHIP_ROWS, HD), F32))
        attended_rows[...] = attended.astype(BF16)
        keep["attended"] = [
            net.copy(attended_rows.at[other_rows, :], att_pair.at[core], net.sibling)
        ]
        att_pair[core] = attended_rows[own_rows, :]

    def project():
        for made in loads:
            made.wait()
        wait_for("attended")
        for n in range(4):
            columns = pl.ds(n * 512, 512)
            partial[:, columns] = (
                jnp.dot(att_pair[0], ow_ref[:128, columns], preferred_element_type=F32)
                + jnp.dot(att_pair[1], ow_ref[128:, columns], preferred_element_type=F32)
            ).astype(BF16)
        exchange_slots("projected", partial, pieces)

    def inverse_norm():
        wide = hidden_rows[...]
        return lax.rsqrt(jnp.mean(wide * wide, axis=1, keepdims=True) + EPSILON)

    def norm():
        wait_for("projected")
        projected = pieces[0:ROWS, :].astype(F32)
        for j in range(1, N_EXP):
            projected = projected + pieces[j * ROWS : (j + 1) * ROWS, :].astype(F32)
        hidden = (residual_ref[...].astype(F32) + projected).astype(BF16)
        hidden_rows[...] = hidden.astype(F32)
        normed = (hidden_rows[...] * inverse_norm() * gain_ref[...]).astype(BF16)

        def rows_of(quarter, columns):
            hot = one_hot(found[0], quarter) + one_hot(found[1], quarter)
            return lax.dot_general(hot, normed[:, columns], TN, preferred_element_type=F32)

        pack(0, rows_of)
        exchange_slots("arrived0", packed.at[0], arrived.at[0])

    def block(ref, e, part):
        full = lambda r: ref.at[e, pl.ds(r * ROWS, ROWS), pl.ds(part * D, D)]
        half = lambda r, h: ref.at[
            e, pl.ds(r * ROWS, ROWS), pl.ds(part * D + h * CHUNK, CHUNK)
        ]
        return full, half

    parts = [(e, part) for e in range(2) for part in range(2)]
    gathers = [gather_steps(net, *block(slots, e, part)) for e, part in parts]
    reduces = []
    for i, (e, part) in enumerate(parts):
        buffers = [ref.at[i] for ref in (far_y, near_y, far_z, near_z)]
        reduces.append(reduce_steps(net, *block(sums, e, part), *buffers))

    def compute_steps(e):
        def enter(half):
            inputs = slots[e, :, :D]
            gate = lax.dot_general(inputs, gates[half, e], NT, preferred_element_type=F32)
            up = lax.dot_general(inputs, ups[half, e], NT, preferred_element_type=F32)
            gate_part[e, half] = gate
            up_part[e, half] = up
            actives[e, half] = (gate * jax.nn.sigmoid(gate) * up).astype(BF16)

        def enter_grad(half):
            grad = lax.dot_general(
                slots[e, :, D:], downs[half, e], NT, preferred_element_type=F32
            )
            gate, up = gate_part[e, half], up_part[e, half]
            s = jax.nn.sigmoid(gate)
            grad_gates[e, half] = (grad * up * s * (1.0 + gate * (1.0 - s))).astype(BF16)
            grad_ups[e, half] = (grad * gate * s).astype(BF16)

        def leave(n, start, terms):
            columns = pl.ds(n * 512, 512)
            total = jnp.zeros((CHIP_ROWS, 512), F32)
            for half in range(2):
                for rows, matrix in terms:
                    total = total + jnp.dot(
                        rows[e, half], matrix[half, e, :, columns], preferred_element_type=F32
                    )
            sums[e, :, pl.ds(start + n * 512, 512)] = total.astype(BF16)

        out_terms = [(actives, downs)]
        grad_terms = [(grad_gates, gates), (grad_ups, ups)]
        steps = [lambda half=half: enter(half) for half in range(2)]
        steps += [lambda half=half: enter_grad(half) for half in range(2)]
        steps += [lambda n=n: leave(n, 0, out_terms) for n in range(4)]
        steps += [lambda n=n: leave(n, D, grad_terms) for n in range(4)]
        return steps

    def pack_sums(part):
        def rows_of(quarter, columns):
            low = part * D + quarter * QUARTER
            both = [sums[e, 0:ROWS, low : low + QUARTER] for e in range(2)]
            return jnp.dot(
                packing(quarter, True),
                jnp.concatenate(both, axis=0),
                preferred_element_type=F32,
            )

        pack(2 + part, rows_of)
        exchange_slots("returned%d" % part, packed.at[2 + part], returned.at[part])

    def pick(k, part):
        rows = [
            jnp.dot(one_hot(found[k], quarter), returned[part], preferred_element_type=F32)
            for quarter in range(4)
        ]
        return jnp.concatenate(rows, axis=1)

    def residual_gradient():
        wait_for("returned1")
        wide, inverse = hidden_rows[...], inverse_norm()
        scaled = gain_ref[...] * (pick(0, 1) + pick(1, 1))
        cube = inverse * inverse * inverse
        grad_hidden = go_ref[...].astype(F32) + (
            inverse * scaled - wide * cube * jnp.mean(wide * scaled, axis=1, keepdims=True)
        )
        residual_out[...] = grad_hidden.astype(BF16)
        keep["slab"] = net.push(lambda peer: residual_out, piece(slab, me))
        piece(slab, me)[...] = residual_out[...]

    def layer_output():
        wait_for("returned0")
        mixture = weight[0] * pick(0, 0) + weight[1] * pick(1, 0)
        layer_out[...] = (hidden_rows[...] + mixture).astype(BF16)

    def attended_gradient():
        wait_for("slab")
        for head in range(2):
            grads[head] = lax.dot_general(
                slab[...],
                ow_ref[head * 128 : head * 128 + 128, :],
                NT,
                preferred_element_type=F32,
            ).astype(BF16)
        keep["grads"] = [net.copy(grads.at[1 - core], grad_heads.at[own_rows, :], net.sibling)]
        grad_heads[own_rows, :] = grads[core]

    def row_delta():
        wait_for("grads")
        delta_rows[...] = jnp.sum(
            grad_heads[...].astype(F32) * attended_rows[...].astype(F32), axis=1, keepdims=True
        )
        dq_rows[...] = jnp.zeros((CHIP_ROWS, HD), F32)

    def back(r):
        low, grad_head = softmax[r], grad_heads[...]
        grad_prob = lax.dot_general(grad_head, kv[r, 256:, :], NT, preferred_element_type=F32)
        grad_score = (low.astype(F32) * (grad_prob - delta_rows[...])).astype(BF16)
        dq_rows[...] += jnp.dot(grad_score, kv[r, :256, :], preferred_element_type=F32)
        grad_sums[r, :256, :] = (
            lax.dot_general(grad_score, queries[...], TN, preferred_element_type=F32) * SCALE
        ).astype(BF16)
        grad_sums[r, 256:, :] = lax.dot_general(
            low, grad_head, TN, preferred_element_type=F32
        ).astype(BF16)

    def send_queries():
        dq_other[...] = (dq_rows[other_rows, :] * SCALE).astype(BF16)
        keep["queries"] = [net.copy(dq_other, pairs.at[0, core], net.sibling)]
        pairs[0, core] = (dq_rows[own_rows, :] * SCALE).astype(BF16)

    def key_sums(i):
        full = lambda r: grad_sums.at[r, pl.ds(i * 256, 256), :]
        half = lambda r, h: grad_sums.at[r, pl.ds(i * 256 + h * 128, 128), :]
        buffers = [ref.at[i] for ref in (att_far_y, att_near_y, att_far_z, att_near_z)]
        return reduce_steps(net, full, half, *buffers)

    for made in exchange:
        made.wait_recv()
    run(
        ORDER,
        [pair(0, score_block), pair(256, lambda r: None)]
        + gathers
        + [compute_steps(e) for e in range(2)]
        + reduces
        + [[lambda r=r: back(r) for r in range(CHIPS)], key_sums(0), key_sums(1)]
        + [[lambda i=i: raise_blocks(i) for i in range(4)]]
        + [
            [
                lambda: score_block(0),
                send_weights,
                dispatch_weighted,
                lambda: unpack(1),
                attend,
                project,
                norm,
                lambda: unpack(0),
                lambda: wait_for("weights"),
                lambda: pack_sums(1),
                residual_gradient,
                attended_gradient,
                row_delta,
                lambda: pack_sums(0),
                layer_output,
                send_queries,
            ]
        ],
    )
    swaps = [
        net.copy(grad_sums.at[0, other_rows, :], pairs.at[1, core], net.sibling),
        net.copy(grad_sums.at[0, other_values, :], pairs.at[2, core], net.sibling),
    ]
    pairs[1, core] = grad_sums[0, own_rows, :]
    pairs[2, core] = grad_sums[0, own_values, :]
    net.finish()
    for made in swaps + keep.pop("queries"):
        made.wait_recv()


def finish_kernel(pairs, layer_ref, residual_ref, layer_out, residual_out, *outs):
    layer_out[...] = layer_ref[...]
    residual_out[...] = residual_ref[...]
    for i, out in enumerate(outs):
        out[:, :128] = pairs[i, 0]
        out[:, 128:] = pairs[i, 1]


def local(
    residual,
    query_states,
    key_states,
    value_states,
    out_weight,
    norm_gain,
    expert_ids,
    gate_weights,
    gate_matrix,
    up_matrix,
    down_matrix,
    grad_out,
):
    inputs = (
        query_states,
        key_states,
        value_states,
        residual,
        norm_gain.reshape(1, D),
        expert_ids.T,
        gate_weights.T,
        grad_out,
        out_weight,
        gate_matrix.transpose(0, 2, 1),
        up_matrix.transpose(0, 2, 1),
        down_matrix,
    )
    v = lambda *shape: pltpu.VMEM(shape, BF16)
    vmem = pl.BlockSpec(memory_space=pltpu.VMEM)
    results = [(ROWS, D), (ROWS, D), (3, 2, 128, HD)]
    layer_out, grad_residual, pairs = pl.pallas_call(
        layer_kernel,
        out_shape=[jax.ShapeDtypeStruct(shape, BF16) for shape in results],
        in_specs=[vmem] * 8 + [pl.BlockSpec(memory_space=pl.ANY)] * 4,
        out_specs=[vmem] * 3,
        scratch_shapes=[
            v(256, D),
            v(CHIP_ROWS, HD),
            v(CHIPS, 512, HD),
            v(CHIPS, CHIP_ROWS, CHIP_ROWS),
            v(CHIP_ROWS, HD),
            pltpu.VMEM((CHIPS, CHIP_ROWS, CHIP_ROWS), F32),
            pltpu.VMEM((CHIP_ROWS, 128), F32),
            pltpu.VMEM((CHIP_ROWS, 128), F32),
            v(2, 128, HD),
            v(128, D),
            v(128, D),
            v(4, 128, QUARTER),
            v(2, 128, QUARTER),
            v(2, CHIP_ROWS, 2 * D),
            v(2, CHIP_ROWS, 2 * D),
            v(2, 2, HIDDEN, D),
            v(2, 2, HIDDEN, D),
            v(2, 2, HIDDEN, D),
            pltpu.VMEM((2, 2, CHIP_ROWS, HIDDEN), F32),
            pltpu.VMEM((2, 2, CHIP_ROWS, HIDDEN), F32),
            v(2, 2, CHIP_ROWS, HIDDEN),
            v(2, 2, CHIP_ROWS, HIDDEN),
            v(2, 2, CHIP_ROWS, HIDDEN),
            v(4, 2, 2, ROWS, CHUNK),
            v(4, 2, 4, ROWS, D),
            v(4, 2, ROWS, CHUNK),
            v(4, 4, ROWS, D),
            v(2, 128, QUARTER),
            pltpu.VMEM((ROWS, D), F32),
            pltpu.VMEM((CHIP_ROWS, 1), F32),
            v(128, D),
            v(2, 128, HD),
            v(CHIP_ROWS, HD),
            v(CHIPS, 512, HD),
            pltpu.VMEM((CHIP_ROWS, HD), F32),
            v(128, HD),
            v(2, 2, 2, 128, HD),
            v(2, 2, 4, 256, HD),
            v(2, 2, 128, HD),
            v(2, 4, 256, HD),
            pltpu.SemaphoreType.DMA((4,)),
            pltpu.SemaphoreType.DMA((COPIES,)),
            pltpu.SemaphoreType.DMA((COPIES,)),
        ],
        compiler_params=pltpu.CompilerParams(
            collective_id=0, has_side_effects=True, vmem_limit_bytes=VMEM_LIMIT
        ),
        cost_estimate=pl.CostEstimate(
            flops=8 * 10**9, bytes_accessed=1 << 24, transcendentals=1 << 21
        ),
    )(*inputs)
    shapes = [(ROWS, D)] * 2 + [(128, 2 * HD)] * 3
    return pl.pallas_call(
        finish_kernel,
        out_shape=[jax.ShapeDtypeStruct(shape, BF16) for shape in shapes],
    )(pairs, layer_out, grad_residual)


def solution(mesh):
    in_specs = (
        P(("ctx", "exp"), None),
        P("ctx", "exp"),
        P("ctx", "exp"),
        P("ctx", "exp"),
        P("exp", None),
        P(),
        P(("ctx", "exp"), None),
        P(("ctx", "exp"), None),
        P("exp", None, "ctx"),
        P("exp", None, "ctx"),
        P("exp", "ctx", None),
        P(("ctx", "exp"), None),
    )
    out_specs = (
        P(("ctx", "exp"), None),
        P(("ctx", "exp"), None),
        P("ctx", "exp"),
        P("ctx", "exp"),
        P("ctx", "exp"),
    )
    return jax.shard_map(local, mesh=mesh, in_specs=in_specs, out_specs=out_specs, check_vma=False)
```

```python
import math

import jax
import jax.numpy as jnp
from jax import lax
from jax.experimental import pallas as pl
from jax.experimental.pallas import tpu as pltpu
from jax.sharding import PartitionSpec as P

MESH = pl.DeviceIdType.MESH
F32 = jnp.float32
BF16 = jnp.bfloat16
HD = 128
D = 2048
ROWS = 16
CHIPS = 16
N_EXP = 8
CHIP_ROWS = 256
HIDDEN = 200
CHUNK = 1024
QUARTER = 512
EPSILON = 1e-05
MASKED = -1e30
SCALE = 1.0 / math.sqrt(HD)
VMEM_LIMIT = 58 * 1024 * 1024
COPIES = 488

ORDER = (
    0, 1, 16, 17, 33, 49, 448, 48, 32, 465, 2, 18, 3, 4, 50, 20, 449, 19, 451, 34, 452, 460, 51, 52,
    8, 7, 36, 35, 21, 5, 456, 24, 453, 461, 6, 37, 53, 22, 466, 96, 160, 54, 112, 450, 55, 38, 23,
    455, 39, 40, 9, 463, 25, 97, 27, 462, 161, 28, 454, 176, 56, 11, 12, 457, 41, 57, 459, 43, 44,
    10, 26, 458, 435, 434, 433, 432, 59, 58, 60, 42, 467, 164, 99, 163, 100, 468, 162, 113, 177,
    103, 116, 464, 98, 166, 102, 114, 179, 115, 180, 178, 165, 101, 469, 182, 117, 185, 181, 118,
    169, 105, 470, 64, 81, 80, 145, 128, 65, 124, 144, 129, 121, 82, 104, 146, 66, 106, 67, 188, 68,
    83, 84, 122, 186, 131, 132, 69, 167, 85, 130, 187, 70, 86, 147, 148, 119, 72, 183, 171, 123,
    136, 87, 107, 149, 184, 170, 134, 73, 168, 89, 133, 108, 471, 88, 92, 150, 152, 76, 120, 91,
    172, 75, 151, 137, 71, 135, 74, 90, 192, 193, 194, 195, 153, 201, 200, 257, 140, 139, 203, 138,
    256, 155, 202, 272, 273, 259, 156, 154, 209, 208, 210, 260, 211, 219, 218, 337, 276, 217, 216,
    321, 336, 275, 258, 263, 320, 196, 340, 199, 324, 279, 261, 274, 214, 281, 264, 339, 265, 343,
    338, 277, 341, 327, 322, 323, 267, 266, 198, 283, 280, 282, 325, 197, 225, 262, 344, 346, 345,
    347, 278, 328, 330, 329, 331, 342, 215, 213, 326, 240, 212, 304, 242, 305, 224, 290, 289, 268,
    269, 307, 284, 241, 306, 285, 228, 332, 348, 349, 333, 472, 308, 292, 288, 245, 226, 231, 244,
    309, 311, 227, 243, 295, 473, 229, 310, 248, 296, 291, 313, 293, 247, 246, 297, 315, 249, 316,
    312, 314, 298, 294, 299, 474, 233, 300, 251, 235, 232, 234, 250, 230, 252, 475, 362, 401, 385,
    369, 363, 361, 400, 384, 417, 359, 358, 366, 404, 416, 354, 388, 367, 372, 357, 420, 368, 387,
    360, 371, 403, 301, 407, 317, 365, 236, 237, 391, 402, 253, 386, 418, 375, 389, 370, 423, 476,
    353, 421, 419, 355, 409, 411, 408, 410, 393, 405, 373, 392, 395, 394, 356, 377, 364, 379, 390,
    424, 426, 376, 422, 378, 425, 427, 406, 374, 352, 478, 428, 396, 397, 477, 412, 413, 380, 381,
    429,
)
NT = (((1,), (1,)), ((), ()))
TN = (((0,), (0,)), ((), ()))


def rel(dy, dz):
    return dy * 4 + dz


class Net:
    def __init__(self, send, recv):
        self.send, self.recv, self.count, self.started = send, recv, 0, []
        ctx = lax.axis_index("ctx")
        self.exp = lax.axis_index("exp")
        self.core = lax.rem(ctx, 2)
        chip = ctx // 2
        self.y, self.z = chip // 4, lax.rem(chip, 4)
        at = lambda y, z, c: {"ctx": (lax.rem(y, 4) * 4 + lax.rem(z, 4)) * 2 + c}
        self.yp = at(self.y + 1, self.z, self.core)
        self.ym = at(self.y + 3, self.z, self.core)
        self.zp = at(self.y, self.z + 1, self.core)
        self.zm = at(self.y, self.z + 3, self.core)
        self.sibling = at(self.y, self.z, 1 - self.core)
        self.peers = [lax.rem(self.exp + d, N_EXP) for d in range(1, N_EXP)]

    def copy(self, src, dst, device):
        i = self.count
        self.count += 1
        made = pltpu.make_async_remote_copy(
            src_ref=src,
            dst_ref=dst,
            send_sem=self.send.at[i],
            recv_sem=self.recv.at[i],
            device_id=device,
            device_id_type=MESH,
        )
        made.start()
        self.started.append(made)
        return made

    def wait(self, made):
        for _ in range(3):
            if len(self.started) > 48:
                self.started.pop(0).wait_send()
        made.wait_recv()

    def finish(self):
        for made in self.started:
            made.wait_send()

    def barrier(self, devices):
        sem = pltpu.get_barrier_semaphore()
        for device in devices:
            pl.semaphore_signal(sem, inc=1, device_id=device, device_id_type=MESH)
        pl.semaphore_wait(sem, len(devices))

    def ring_devices(self):
        return [self.yp, self.ym, self.zp, self.zm]

    def peer_devices(self):
        return [{"exp": peer} for peer in self.peers]

    def push(self, src_of, dst):
        return [self.copy(src_of(peer), dst, {"exp": peer}) for peer in self.peers]


def gather_steps(net, full, half):
    state = {}

    def send_z():
        state["z3"] = net.copy(full(rel(0, 0)), full(rel(0, 3)), net.zp)
        state["z1"] = net.copy(full(rel(0, 0)), full(rel(0, 1)), net.zm)

    def send_y(dz):
        state["y3", dz] = net.copy(full(rel(0, dz)), full(rel(3, dz)), net.yp)
        state["y1", dz] = net.copy(full(rel(0, dz)), full(rel(1, dz)), net.ym)

    def near_z3():
        net.wait(state["z3"])
        state["h0"] = net.copy(half(rel(0, 3), 0), half(rel(0, 2), 0), net.zp)
        send_y(3)

    def near_z1():
        net.wait(state["z1"])
        state["h1"] = net.copy(half(rel(0, 1), 1), half(rel(0, 2), 1), net.zm)
        send_y(1)

    def far_z():
        net.wait(state["h0"])
        net.wait(state["h1"])
        send_y(2)

    def near_y(dz):
        net.wait(state["y3", dz])
        net.wait(state["y1", dz])
        if dz in (0, 2):
            state["g0", dz] = net.copy(half(rel(3, dz), 0), half(rel(2, dz), 0), net.yp)
            state["g1", dz] = net.copy(half(rel(1, dz), 1), half(rel(2, dz), 1), net.ym)

    def far_y(dz):
        net.wait(state["g0", dz])
        net.wait(state["g1", dz])
        if dz == 0:
            state["f3"] = net.copy(full(rel(2, 0)), full(rel(2, 3)), net.zp)
            state["f1"] = net.copy(full(rel(2, 0)), full(rel(2, 1)), net.zm)

    def end(dz):
        net.wait(state["f%d" % dz])

    return [
        send_z,
        lambda: send_y(0),
        lambda: near_y(0),
        near_z3,
        near_z1,
        lambda: far_y(0),
        far_z,
        lambda: near_y(3),
        lambda: near_y(1),
        lambda: near_y(2),
        lambda: far_y(2),
        lambda: end(3),
        lambda: end(1),
    ]


def reduce_steps(net, full, half, far_y, near_y, far_z, near_z):
    ra, rb, za, zb = far_y.at[0], far_y.at[1], far_z.at[0], far_z.at[1]
    rc, rd = near_y.at[0], near_y.at[1]
    zc, zd, ze, zf = [near_z.at[i] for i in range(4)]
    state = {}

    def add(target, *sources):
        total = target[...].astype(F32)
        for source in sources:
            total = total + source[...].astype(F32)
        target[...] = total.astype(BF16)

    def send_far_z():
        state["e"] = net.copy(full(rel(2, 1)), ze, net.zp)
        state["f"] = net.copy(full(rel(2, 3)), zf, net.zm)

    def send_far_y(dz):
        if dz == 0:
            net.wait(state["e"])
            net.wait(state["f"])
            add(full(rel(2, 0)), ze, zf)
        state["a", dz] = net.copy(half(rel(2, dz), 0), ra.at[dz // 2], net.yp)
        state["b", dz] = net.copy(half(rel(2, dz), 1), rb.at[dz // 2], net.ym)

    def send_near(dz):
        if dz in (0, 2):
            net.wait(state["a", dz])
            net.wait(state["b", dz])
            add(half(rel(1, dz), 0), ra.at[dz // 2])
            add(half(rel(3, dz), 1), rb.at[dz // 2])
        state["c", dz] = net.copy(full(rel(1, dz)), rc.at[dz], net.yp)
        state["d", dz] = net.copy(full(rel(3, dz)), rd.at[dz], net.ym)

    def collect(dz):
        net.wait(state["c", dz])
        net.wait(state["d", dz])
        add(full(rel(0, dz)), rc.at[dz], rd.at[dz])
        if dz == 2:
            state["za"] = net.copy(half(rel(0, 2), 0), za, net.zp)
            state["zb"] = net.copy(half(rel(0, 2), 1), zb, net.zm)

    def send_z1():
        net.wait(state["za"])
        add(half(rel(0, 1), 0), za)
        state["zc"] = net.copy(full(rel(0, 1)), zc, net.zp)

    def send_z3():
        net.wait(state["zb"])
        add(half(rel(0, 3), 1), zb)
        state["zd"] = net.copy(full(rel(0, 3)), zd, net.zm)

    def last():
        net.wait(state["zc"])
        net.wait(state["zd"])
        add(full(rel(0, 0)), zc, zd)

    return [
        send_far_z,
        lambda: send_far_y(2),
        lambda: send_near(1),
        lambda: send_near(3),
        lambda: send_near(2),
        lambda: send_far_y(0),
        lambda: send_near(0),
        lambda: collect(2),
        lambda: collect(1),
        lambda: collect(3),
        send_z1,
        send_z3,
        lambda: collect(0),
        last,
    ]


def run(order, parts):
    assert sorted(order) == [16 * p + s for p, part in enumerate(parts) for s in range(len(part))]
    for code in order:
        parts[code // 16][code % 16]()


def column(ref, k):
    diagonal = lax.broadcasted_iota(jnp.int32, (ROWS, ROWS), 0) == lax.broadcasted_iota(
        jnp.int32, (ROWS, ROWS), 1
    )
    row = jnp.broadcast_to(ref[k : k + 1, :], (ROWS, ROWS))
    return jnp.sum(jnp.where(diagonal, row, jnp.zeros_like(row)), axis=1, keepdims=True)


def places(ids_ref):
    lanes = lax.broadcasted_iota(jnp.int32, (ROWS, 128), 1)
    ids = [column(ids_ref, k) for k in range(2)]
    chosen = [(lanes == one).astype(F32) for one in ids]
    lower = (
        lax.broadcasted_iota(jnp.int32, (ROWS, ROWS), 1)
        < lax.broadcasted_iota(jnp.int32, (ROWS, ROWS), 0)
    ).astype(BF16)
    earlier = jnp.dot(lower, (chosen[0] + chosen[1]).astype(BF16), preferred_element_type=F32)
    found = []
    for one, hot in zip(ids, chosen):
        rank = jnp.sum(earlier * hot, axis=1, keepdims=True).astype(jnp.int32)
        place = (one >> 1) * 16 + (one & 1) * 2 + rank
        found.append(jnp.where(rank < 2, place, -1000))
    return found


def one_hot(place, quarter):
    lanes = lax.broadcasted_iota(jnp.int32, (ROWS, 128), 1)
    return (lanes == place + 4 * quarter).astype(BF16)


def packing(quarter, transposed):
    shape, slot_dim = ((128, 32), 1) if transposed else ((32, 128), 0)
    slot = lax.broadcasted_iota(jnp.int32, shape, slot_dim)
    packed = lax.broadcasted_iota(jnp.int32, shape, 1 - slot_dim)
    want = ((slot & 15) >> 1) * 16 + quarter * 4 + (slot >> 4) * 2 + (slot & 1)
    return (packed == want).astype(BF16)


def layer_kernel(
    q_ref,
    k_ref,
    v_ref,
    residual_ref,
    gain_ref,
    ids_ref,
    gw_ref,
    go_ref,
    ow_hbm,
    wg_hbm,
    wu_hbm,
    wd_hbm,
    layer_out,
    residual_out,
    pairs,
    ow_ref,
    queries,
    kv,
    softmax,
    attended_rows,
    scores,
    row_top,
    row_sum,
    att_pair,
    partial,
    pieces,
    packed,
    arrived,
    slots,
    sums,
    gates,
    ups,
    downs,
    gate_part,
    up_part,
    actives,
    grad_gates,
    grad_ups,
    far_y,
    near_y,
    far_z,
    near_z,
    returned,
    hidden_rows,
    delta_rows,
    slab,
    grads,
    grad_heads,
    grad_sums,
    dq_rows,
    dq_other,
    att_far_y,
    att_near_y,
    att_far_z,
    att_near_z,
    load_sem,
    send,
    recv,
):
    net = Net(send, recv)
    core, me = net.core, net.exp
    own_rows = pl.ds(pl.multiple_of(core * 128, 128), 128)
    other_rows = pl.ds(pl.multiple_of((1 - core) * 128, 128), 128)
    own_values = pl.ds(pl.multiple_of(256 + core * 128, 128), 128)
    other_values = pl.ds(pl.multiple_of(256 + (1 - core) * 128, 128), 128)

    def piece(ref, peer):
        return ref.at[pl.ds(pl.multiple_of(peer * ROWS, ROWS), ROWS), :]

    def mine(ref):
        return jnp.where(core == 0, ref[:, :128], ref[:, 128:])

    weights = ((wg_hbm, gates), (wu_hbm, ups), (wd_hbm, downs))
    loads = [pltpu.make_async_copy(ow_hbm, ow_ref, load_sem.at[0])]
    for i, (source, target) in enumerate(weights):
        loads.append(pltpu.make_async_copy(source, target.at[0], load_sem.at[i + 1]))
    for made in loads:
        made.start()
    net.barrier(net.ring_devices() + [net.sibling] + net.peer_devices())

    exchange = [
        net.copy(k_ref.at[:, other_rows], kv.at[0, own_rows, :], net.sibling),
        net.copy(q_ref.at[:, other_rows], queries.at[own_rows, :], net.sibling),
        net.copy(v_ref.at[:, other_rows], kv.at[0, own_values, :], net.sibling),
    ]
    kv[0, own_rows, :] = mine(k_ref)
    kv[0, own_values, :] = mine(v_ref)
    queries[own_rows, :] = mine(q_ref)

    chip = net.y * 4 + net.z

    def score_block(r):
        dy, dz = r // 4, r % 4
        other = lax.rem(net.y + dy, 4) * 4 + lax.rem(net.z + dz, 4)
        s = lax.dot_general(queries[...], kv[r, :256, :], NT, preferred_element_type=F32) * SCALE
        row = lax.broadcasted_iota(jnp.int32, (CHIP_ROWS, CHIP_ROWS), 0) + chip * CHIP_ROWS
        place = lax.broadcasted_iota(jnp.int32, (CHIP_ROWS, CHIP_ROWS), 1) + other * CHIP_ROWS
        s = jnp.where(place <= row, s, MASKED)
        scores[r] = s
        row_top[...] = jnp.maximum(row_top[...], jnp.maximum(s[:, :128], s[:, 128:]))

    row_top[...] = jnp.full((CHIP_ROWS, 128), MASKED, F32)
    row_sum[...] = jnp.zeros((CHIP_ROWS, 128), F32)

    def raise_blocks(quarter):
        m = jnp.max(row_top[...], axis=1, keepdims=True)

        def one(r, total):
            e = jnp.exp(scores[r] - m)
            scores[r] = e
            return total + (e[:, :128] + e[:, 128:])

        row_sum[...] = lax.fori_loop(4 * quarter, 4 * quarter + 4, one, row_sum[...])

    def key_block(ref, i):
        full = lambda r: ref.at[r, pl.ds(i * 128, 128), :]
        half = lambda r, h: ref.at[r, pl.ds(i * 128 + h * 64, 64), :]
        return full, half

    keep = {}

    def send_weights():
        keep["weights"] = [net.copy(hbm, at.at[1], net.sibling) for hbm, at in weights]

    def wait_for(name):
        for made in keep.pop(name):
            net.wait(made)

    found = places(ids_ref)
    weight = [column(gw_ref, k) for k in range(2)]

    def exchange_slots(name, source, target):
        keep[name] = net.push(lambda peer: piece(source, peer), piece(target, me))
        piece(target, me)[...] = piece(source, me)[...]

    def pack(part, rows_of):
        for quarter in range(4):
            columns = slice(quarter * QUARTER, (quarter + 1) * QUARTER)
            spread = rows_of(quarter, columns)
            total = spread if quarter == 0 else total + spread
        packed[part] = total.astype(BF16)

    def dispatch_weighted():
        grad_out = go_ref[...].astype(F32)
        weighted = [(weight[k] * grad_out).astype(BF16) for k in range(2)]

        def rows_of(quarter, columns):
            return sum(
                lax.dot_general(
                    one_hot(found[k], quarter),
                    weighted[k][:, columns],
                    TN,
                    preferred_element_type=F32,
                )
                for k in range(2)
            )

        pack(1, rows_of)
        exchange_slots("arrived1", packed.at[1], arrived.at[1])

    def unpack(part):
        wait_for("arrived%d" % part)
        for quarter in range(4):
            rows = jnp.dot(packing(quarter, False), arrived[part], preferred_element_type=F32)
            rows = rows.astype(BF16)
            low = part * D + quarter * QUARTER
            for e in range(2):
                slots[e, 0:ROWS, low : low + QUARTER] = rows[e * ROWS : (e + 1) * ROWS]

    def attend():
        inverse = 1.0 / jnp.sum(row_sum[...], axis=1, keepdims=True)

        def one(r, acc):
            low = (scores[r] * inverse).astype(BF16)
            softmax[r] = low
            return acc + jnp.dot(low, kv[r, 256:, :], preferred_element_type=F32)

        attended = lax.fori_loop(0, CHIPS, one, jnp.zeros((CHIP_ROWS, HD), F32))
        attended_rows[...] = attended.astype(BF16)
        keep["attended"] = [
            net.copy(attended_rows.at[other_rows, :], att_pair.at[core], net.sibling)
        ]
        att_pair[core] = attended_rows[own_rows, :]

    def project():
        for made in loads:
            made.wait()
        wait_for("attended")
        for n in range(4):
            columns = pl.ds(n * 512, 512)
            partial[:, columns] = (
                jnp.dot(att_pair[0], ow_ref[:128, columns], preferred_element_type=F32)
                + jnp.dot(att_pair[1], ow_ref[128:, columns], preferred_element_type=F32)
            ).astype(BF16)
        exchange_slots("projected", partial, pieces)

    def inverse_norm():
        wide = hidden_rows[...]
        return lax.rsqrt(jnp.mean(wide * wide, axis=1, keepdims=True) + EPSILON)

    def norm():
        wait_for("projected")
        projected = pieces[0:ROWS, :].astype(F32)
        for j in range(1, N_EXP):
            projected = projected + pieces[j * ROWS : (j + 1) * ROWS, :].astype(F32)
        hidden = (residual_ref[...].astype(F32) + projected).astype(BF16)
        hidden_rows[...] = hidden.astype(F32)
        normed = (hidden_rows[...] * inverse_norm() * gain_ref[...]).astype(BF16)

        def rows_of(quarter, columns):
            hot = one_hot(found[0], quarter) + one_hot(found[1], quarter)
            return lax.dot_general(hot, normed[:, columns], TN, preferred_element_type=F32)

        pack(0, rows_of)
        exchange_slots("arrived0", packed.at[0], arrived.at[0])

    def block(ref, i):
        e, low = i // 4, i % 4 * CHUNK
        full = lambda r: ref.at[e, pl.ds(r * ROWS, ROWS), pl.ds(low, CHUNK)]
        half = lambda r, h: ref.at[
            e, pl.ds(r * ROWS, ROWS), pl.ds(low + h * QUARTER, QUARTER)
        ]
        return full, half

    gathers = [gather_steps(net, *block(slots, i)) for i in range(8)]
    reduces = []
    for i in range(8):
        buffers = [ref.at[i] for ref in (far_y, near_y, far_z, near_z)]
        reduces.append(reduce_steps(net, *block(sums, i), *buffers))

    def compute_steps(e):
        def enter(half):
            inputs = slots[e, :, :D]
            gate = lax.dot_general(inputs, gates[half, e], NT, preferred_element_type=F32)
            up = lax.dot_general(inputs, ups[half, e], NT, preferred_element_type=F32)
            gate_part[e, half] = gate
            up_part[e, half] = up
            actives[e, half] = (gate * jax.nn.sigmoid(gate) * up).astype(BF16)

        def enter_grad(half):
            grad = lax.dot_general(
                slots[e, :, D:], downs[half, e], NT, preferred_element_type=F32
            )
            gate, up = gate_part[e, half], up_part[e, half]
            s = jax.nn.sigmoid(gate)
            grad_gates[e, half] = (grad * up * s * (1.0 + gate * (1.0 - s))).astype(BF16)
            grad_ups[e, half] = (grad * gate * s).astype(BF16)

        def leave(n, start, terms):
            columns = pl.ds(n * 512, 512)
            total = jnp.zeros((CHIP_ROWS, 512), F32)
            for half in range(2):
                for rows, matrix in terms:
                    total = total + jnp.dot(
                        rows[e, half], matrix[half, e, :, columns], preferred_element_type=F32
                    )
            sums[e, :, pl.ds(start + n * 512, 512)] = total.astype(BF16)

        out_terms = [(actives, downs)]
        grad_terms = [(grad_gates, gates), (grad_ups, ups)]
        steps = [lambda half=half: enter(half) for half in range(2)]
        steps += [lambda half=half: enter_grad(half) for half in range(2)]
        steps += [lambda n=n: leave(n, 0, out_terms) for n in range(4)]
        steps += [lambda n=n: leave(n, D, grad_terms) for n in range(4)]
        return steps

    def pack_sums(part):
        def rows_of(quarter, columns):
            low = part * D + quarter * QUARTER
            both = [sums[e, 0:ROWS, low : low + QUARTER] for e in range(2)]
            return jnp.dot(
                packing(quarter, True),
                jnp.concatenate(both, axis=0),
                preferred_element_type=F32,
            )

        pack(2 + part, rows_of)
        exchange_slots("returned%d" % part, packed.at[2 + part], returned.at[part])

    def pick(k, part):
        rows = [
            jnp.dot(one_hot(found[k], quarter), returned[part], preferred_element_type=F32)
            for quarter in range(4)
        ]
        return jnp.concatenate(rows, axis=1)

    def residual_gradient():
        wait_for("returned1")
        wide, inverse = hidden_rows[...], inverse_norm()
        scaled = gain_ref[...] * (pick(0, 1) + pick(1, 1))
        cube = inverse * inverse * inverse
        grad_hidden = go_ref[...].astype(F32) + (
            inverse * scaled - wide * cube * jnp.mean(wide * scaled, axis=1, keepdims=True)
        )
        residual_out[...] = grad_hidden.astype(BF16)
        keep["slab"] = net.push(lambda peer: residual_out, piece(slab, me))
        piece(slab, me)[...] = residual_out[...]

    def layer_output():
        wait_for("returned0")
        mixture = weight[0] * pick(0, 0) + weight[1] * pick(1, 0)
        layer_out[...] = (hidden_rows[...] + mixture).astype(BF16)

    def attended_gradient():
        wait_for("slab")
        for head in range(2):
            grads[head] = lax.dot_general(
                slab[...],
                ow_ref[head * 128 : head * 128 + 128, :],
                NT,
                preferred_element_type=F32,
            ).astype(BF16)
        keep["grads"] = [net.copy(grads.at[1 - core], grad_heads.at[own_rows, :], net.sibling)]
        grad_heads[own_rows, :] = grads[core]

    def row_delta():
        wait_for("grads")
        delta_rows[...] = jnp.sum(
            grad_heads[...].astype(F32) * attended_rows[...].astype(F32), axis=1, keepdims=True
        )
        dq_rows[...] = jnp.zeros((CHIP_ROWS, HD), F32)

    def back(r):
        low, grad_head = softmax[r], grad_heads[...]
        grad_prob = lax.dot_general(grad_head, kv[r, 256:, :], NT, preferred_element_type=F32)
        grad_score = (low.astype(F32) * (grad_prob - delta_rows[...])).astype(BF16)
        dq_rows[...] += jnp.dot(grad_score, kv[r, :256, :], preferred_element_type=F32)
        grad_sums[r, :256, :] = (
            lax.dot_general(grad_score, queries[...], TN, preferred_element_type=F32) * SCALE
        ).astype(BF16)
        grad_sums[r, 256:, :] = lax.dot_general(
            low, grad_head, TN, preferred_element_type=F32
        ).astype(BF16)

    def send_queries():
        dq_other[...] = (dq_rows[other_rows, :] * SCALE).astype(BF16)
        keep["queries"] = [net.copy(dq_other, pairs.at[0, core], net.sibling)]
        pairs[0, core] = (dq_rows[own_rows, :] * SCALE).astype(BF16)

    def key_sums(i):
        buffers = [ref.at[i] for ref in (att_far_y, att_near_y, att_far_z, att_near_z)]
        return reduce_steps(net, *key_block(grad_sums, i), *buffers)

    for made in exchange:
        made.wait_recv()
    run(
        ORDER,
        [gather_steps(net, *key_block(kv, i)) for i in range(4)]
        + gathers
        + [compute_steps(e) for e in range(2)]
        + reduces
        + [[lambda r=r: back(r) for r in range(CHIPS)]]
        + [key_sums(i) for i in range(4)]
        + [[lambda i=i: raise_blocks(i) for i in range(4)]]
        + [[lambda r=r: score_block(r) for r in range(CHIPS)]]
        + [
            [
                send_weights,
                dispatch_weighted,
                lambda: unpack(1),
                attend,
                project,
                norm,
                lambda: unpack(0),
                lambda: wait_for("weights"),
                lambda: pack_sums(1),
                residual_gradient,
                attended_gradient,
                row_delta,
                lambda: pack_sums(0),
                layer_output,
                send_queries,
            ]
        ],
    )
    swaps = [
        net.copy(grad_sums.at[0, other_rows, :], pairs.at[1, core], net.sibling),
        net.copy(grad_sums.at[0, other_values, :], pairs.at[2, core], net.sibling),
    ]
    pairs[1, core] = grad_sums[0, own_rows, :]
    pairs[2, core] = grad_sums[0, own_values, :]
    net.finish()
    for made in swaps + keep.pop("queries"):
        made.wait_recv()


def finish_kernel(pairs, layer_ref, residual_ref, layer_out, residual_out, *outs):
    layer_out[...] = layer_ref[...]
    residual_out[...] = residual_ref[...]
    for i, out in enumerate(outs):
        out[:, :128] = pairs[i, 0]
        out[:, 128:] = pairs[i, 1]


def local(
    residual,
    query_states,
    key_states,
    value_states,
    out_weight,
    norm_gain,
    expert_ids,
    gate_weights,
    gate_matrix,
    up_matrix,
    down_matrix,
    grad_out,
):
    inputs = (
        query_states,
        key_states,
        value_states,
        residual,
        norm_gain.reshape(1, D),
        expert_ids.T,
        gate_weights.T,
        grad_out,
        out_weight,
        gate_matrix.transpose(0, 2, 1),
        up_matrix.transpose(0, 2, 1),
        down_matrix,
    )
    v = lambda *shape: pltpu.VMEM(shape, BF16)
    vmem = pl.BlockSpec(memory_space=pltpu.VMEM)
    results = [(ROWS, D), (ROWS, D), (3, 2, 128, HD)]
    layer_out, grad_residual, pairs = pl.pallas_call(
        layer_kernel,
        out_shape=[jax.ShapeDtypeStruct(shape, BF16) for shape in results],
        in_specs=[vmem] * 8 + [pl.BlockSpec(memory_space=pl.ANY)] * 4,
        out_specs=[vmem] * 3,
        scratch_shapes=[
            v(256, D),
            v(CHIP_ROWS, HD),
            v(CHIPS, 512, HD),
            v(CHIPS, CHIP_ROWS, CHIP_ROWS),
            v(CHIP_ROWS, HD),
            pltpu.VMEM((CHIPS, CHIP_ROWS, CHIP_ROWS), F32),
            pltpu.VMEM((CHIP_ROWS, 128), F32),
            pltpu.VMEM((CHIP_ROWS, 128), F32),
            v(2, 128, HD),
            v(128, D),
            v(128, D),
            v(4, 128, QUARTER),
            v(2, 128, QUARTER),
            v(2, CHIP_ROWS, 2 * D),
            v(2, CHIP_ROWS, 2 * D),
            v(2, 2, HIDDEN, D),
            v(2, 2, HIDDEN, D),
            v(2, 2, HIDDEN, D),
            pltpu.VMEM((2, 2, CHIP_ROWS, HIDDEN), F32),
            pltpu.VMEM((2, 2, CHIP_ROWS, HIDDEN), F32),
            v(2, 2, CHIP_ROWS, HIDDEN),
            v(2, 2, CHIP_ROWS, HIDDEN),
            v(2, 2, CHIP_ROWS, HIDDEN),
            v(8, 2, 2, ROWS, QUARTER),
            v(8, 2, 4, ROWS, CHUNK),
            v(8, 2, ROWS, QUARTER),
            v(8, 4, ROWS, CHUNK),
            v(2, 128, QUARTER),
            pltpu.VMEM((ROWS, D), F32),
            pltpu.VMEM((CHIP_ROWS, 1), F32),
            v(128, D),
            v(2, 128, HD),
            v(CHIP_ROWS, HD),
            v(CHIPS, 512, HD),
            pltpu.VMEM((CHIP_ROWS, HD), F32),
            v(128, HD),
            v(4, 2, 2, 64, HD),
            v(4, 2, 4, 128, HD),
            v(4, 2, 64, HD),
            v(4, 4, 128, HD),
            pltpu.SemaphoreType.DMA((4,)),
            pltpu.SemaphoreType.DMA((COPIES,)),
            pltpu.SemaphoreType.DMA((COPIES,)),
        ],
        compiler_params=pltpu.CompilerParams(
            collective_id=0, has_side_effects=True, vmem_limit_bytes=VMEM_LIMIT
        ),
        cost_estimate=pl.CostEstimate(
            flops=8 * 10**9, bytes_accessed=1 << 24, transcendentals=1 << 21
        ),
    )(*inputs)
    shapes = [(ROWS, D)] * 2 + [(128, 2 * HD)] * 3
    return pl.pallas_call(
        finish_kernel,
        out_shape=[jax.ShapeDtypeStruct(shape, BF16) for shape in shapes],
    )(pairs, layer_out, grad_residual)


def solution(mesh):
    in_specs = (
        P(("ctx", "exp"), None),
        P("ctx", "exp"),
        P("ctx", "exp"),
        P("ctx", "exp"),
        P("exp", None),
        P(),
        P(("ctx", "exp"), None),
        P(("ctx", "exp"), None),
        P("exp", None, "ctx"),
        P("exp", None, "ctx"),
        P("exp", "ctx", None),
        P(("ctx", "exp"), None),
    )
    out_specs = (
        P(("ctx", "exp"), None),
        P(("ctx", "exp"), None),
        P("ctx", "exp"),
        P("ctx", "exp"),
        P("ctx", "exp"),
    )
    return jax.shard_map(local, mesh=mesh, in_specs=in_specs, out_specs=out_specs, check_vma=False)
```
